512 devices in a mesh: row: 8 (over x_hi, y), col: 32 (over x_lo, z), head: 2 (over core).
Axes of the slice: x: 4 (x_hi: 2, x_lo: 2; x = x_hi * 2 + x_lo), y: 4, z: 16, core: 2. Of those that a mesh axis runs over, the one named last changes fastest.
Arguments:
- pair: bfloat16 [32, 4096, 128], P('row', 'col'), may hold values from -6 to 6
- layer_norm_gain: float32 [128], replicated, may hold values from 0.1 to 1.9
- w_proj: bfloat16 [128, 512], P(None, 'head'), may hold values from -0.5 to 0.5
- w_out: bfloat16 [128, 128], P('head'), may hold values from -0.5 to 0.5
- tri_bias: bfloat16 [4, 4096, 4096], P('head', 'col', 'row'), may hold values from -6 to 300
- active: int32 [16, 16], replicated, may hold values from 0 to 1, as said below
- d_out: bfloat16 [32, 4096, 128], P('row', 'col'), may hold values from -6 to 6
Outputs:
- out: bfloat16 [32, 4096, 128], P('row', 'col', 'head')
- pair_gradient: bfloat16 [32, 4096, 128], P('row', 'col')
The draws below stay inside these ranges and needn't reach their ends.
Inputs may be any that keep to these rules, and one draw needn't show every extreme that they name: Entry [a, b] is 1 where key tile b is computed for query tile a; the table is symmetric and every tile is active with itself.
All inputs are finite; a program needn't handle non-finite values.
Results may differ from the reference program's by a relative error of at most 0.02.
Values may be sent and summed in bfloat16 or wider, within the bound.
No kernel may reach another device: no remote copies, remote signals or barrier semaphores. Data moves between devices by JAX's collectives and lax.ppermute only.
A program may use at most 64 MiB of HBM per device.

```python
import jax
import jax.numpy as jnp
from jax import lax

C = 128
H = 4
DH = 32
TILE = 256
COL_DEV = 128
R = 32
N = 4096
NT = 16
N_COL = 32


def draw_tri_bias(key, part):
    key = jax.random.fold_in(key, 11)
    base = jnp.clip(jax.random.normal(key, (H, N, N), jnp.float32), -6.0, 6.0)
    return base.astype(jnp.bfloat16)


def draw_active(key, part):
    key = jax.random.fold_in(key, 23)
    key_weight, key_pick = jax.random.split(key)
    weight = jax.random.randint(key_weight, (NT,), 1, 7)
    pick = jax.random.randint(key_pick, (NT, NT), 0, 25)
    pick = jnp.minimum(pick, pick.T)
    index = jnp.arange(NT, dtype=jnp.int32)
    same = index[:, None] == index[None, :]
    corner = (index[:, None] == 0) & (index[None, :] == NT - 1) | (index[:, None] == NT - 1) & (index[None, :] == 0)
    chosen = same | (pick < weight[:, None] * weight[None, :]) & jnp.logical_not(corner)
    return jnp.where(chosen, 1, 0).astype(jnp.int32)


def block_scale(rng, shape, pieces, smallest, largest):
    gain, own = 1.0, jax.random.fold_in(rng, 6)
    for dim, parts in pieces:
        heights = jnp.exp(jax.random.uniform(jax.random.fold_in(own, dim), (parts,), jnp.float32, smallest / len(pieces), largest / len(pieces)))
        gain = gain * jnp.repeat(heights, shape[dim] // parts).reshape([-1 if axis == dim else 1 for axis in range(len(shape))])
    return gain


def centred(key, extent, scale, bound, pieces=(), kind=jnp.bfloat16):
    drawn = jax.random.normal(key, extent, jnp.float32) * scale
    if len(pieces) > 0:
        drawn = block_scale(key, extent, pieces, -0.22, 0.18) * drawn
    return jnp.clip(drawn, min=-bound, max=bound).astype(kind)


def setup_inputs(seed: int = 0) -> dict:
    splits = jax.random.split(jax.random.key(seed), 8)
    return {
        "pair": centred(splits[0], (R, N, C), 1.0, 6.0, ((0, 8), (1, 32))),
        "layer_norm_gain": jnp.clip(1.0 + 0.18 * jax.random.normal(splits[1], (C,), jnp.float32), 0.1, 1.9),
        "w_proj": centred(splits[2], (C, H * 4 * DH), C ** -0.5, 0.5, ((1, 2),)),
        "w_out": centred(splits[3], (H * DH, C), (H * DH) ** -0.5, 0.5, ((0, 2),)),
        "tri_bias": draw_tri_bias(jax.random.fold_in(splits[7], 71), 0),
        "active": draw_active(jax.random.fold_in(splits[7], 71), 0),
        "d_out": centred(splits[6], (R, N, C), 1.0, 6.0, ((0, 8), (1, 32))),
    }


EPS = 1e-05
NEG = -1e+30

def attend_row(q_row, k_row, v_row, do_row, bias_head, active, tiles):
    scale = DH ** (-0.5)

    def block(carry, number):
        d_keys, d_vals = carry
        start = number * COL_DEV
        q_blk = lax.dynamic_slice_in_dim(q_row, start, COL_DEV, 0)
        bias_blk = lax.dynamic_slice_in_dim(bias_head, start, COL_DEV, 0).astype(jnp.float32)
        tile_blk = lax.dynamic_slice_in_dim(tiles, start, COL_DEV, 0)
        allowed = jnp.take(active, tile_blk, axis=0)[:, tiles] == 1
        score = jnp.dot(q_blk, k_row.T, preferred_element_type=jnp.float32) + bias_blk
        score = jnp.where(allowed, score, NEG)
        top = lax.optimization_barrier(jnp.max(score, axis=1, keepdims=True))
        weights = jnp.where(allowed, jnp.exp(score - top), 0.0)
        total = lax.optimization_barrier(jnp.sum(weights, axis=1, keepdims=True))
        attended = jnp.dot(weights.astype(jnp.bfloat16), v_row, preferred_element_type=jnp.float32) / total
        lse = top + jnp.log(total)
        do_blk = lax.dynamic_slice_in_dim(do_row, start, COL_DEV, 0)
        delta = lax.optimization_barrier(jnp.sum(do_blk * attended, axis=1, keepdims=True))
        grad_blk = do_blk.astype(jnp.bfloat16)
        prob = jnp.where(allowed, jnp.exp(score - lse), 0.0)
        d_value = jnp.dot(prob.astype(jnp.bfloat16).T, grad_blk, preferred_element_type=jnp.float32)
        d_prob = jnp.dot(grad_blk, v_row.T, preferred_element_type=jnp.float32)
        d_score = (prob * (d_prob - delta)).astype(jnp.bfloat16)
        d_query = jnp.dot(d_score, k_row, preferred_element_type=jnp.float32) * scale
        d_key = jnp.dot(d_score.T, q_blk, preferred_element_type=jnp.float32)
        d_keys = d_keys + lax.optimization_barrier(d_key.astype(jnp.bfloat16)).astype(jnp.float32)
        d_vals = d_vals + lax.optimization_barrier(d_value.astype(jnp.bfloat16)).astype(jnp.float32)
        return ((d_keys, d_vals), (attended, d_query))
    zeros = jnp.zeros((N, DH), jnp.float32)
    (d_keys, d_vals), (attended, d_query) = lax.scan(block, (zeros, zeros), jnp.arange(N_COL, dtype=jnp.int32))
    return (attended.reshape(N, DH), d_query.reshape(N, DH), d_keys, d_vals)

def reference(pair, layer_norm_gain, w_proj, w_out, tri_bias, active, d_out):
    x = pair.astype(jnp.float32)
    channel_average = lax.optimization_barrier(jnp.mean(x, axis=-1, keepdims=True))
    centered_input = x - channel_average
    inverse_deviation = lax.rsqrt(lax.optimization_barrier(jnp.mean(centered_input * centered_input, axis=-1, keepdims=True)) + EPS)
    standardized_input = centered_input * inverse_deviation
    normalized_pair = (standardized_input * layer_norm_gain).astype(jnp.bfloat16)
    proj = jnp.einsum('rjc,cf->rjf', normalized_pair.astype(jnp.float32), w_proj.astype(jnp.float32))
    proj = proj.reshape(R, N, H, 4, DH)
    scale = DH ** (-0.5)
    query = (proj[:, :, :, 0] * scale).astype(jnp.bfloat16)
    keys = proj[:, :, :, 1].astype(jnp.bfloat16)
    values = proj[:, :, :, 2].astype(jnp.bfloat16)
    gate = jax.nn.sigmoid(proj[:, :, :, 3])
    d_go = jnp.einsum('rjc,fc->rjf', d_out.astype(jnp.float32), w_out.astype(jnp.float32)).reshape(R, N, H, DH)
    d_o = d_go * gate
    tiles = jnp.arange(N, dtype=jnp.int32) // TILE
    outs_o = []
    outs_dq = []
    outs_dk = []
    outs_dv = []
    for head in range(H):
        bias_head = tri_bias[head]

        def one_row(item, bias_head=bias_head):
            return attend_row(item[0], item[1], item[2], item[3], bias_head, active, tiles)
        attended, d_query, d_keys, d_vals = lax.map(one_row, (query[:, :, head], keys[:, :, head], values[:, :, head], d_o[:, :, head]))
        outs_o.append(attended)
        outs_dq.append(d_query)
        outs_dk.append(d_keys)
        outs_dv.append(d_vals)
    attended = jnp.stack(outs_o, axis=2)
    d_query = jnp.stack(outs_dq, axis=2)
    d_keys = jnp.stack(outs_dk, axis=2)
    d_vals = jnp.stack(outs_dv, axis=2)
    gated = (gate * attended).astype(jnp.bfloat16).reshape(R * N, H * DH)
    out = jnp.dot(gated, w_out, preferred_element_type=jnp.float32).reshape(R, N, C).astype(jnp.bfloat16)
    d_gate = d_go * attended * gate * (1.0 - gate)
    d_proj = jnp.stack([d_query, d_keys, d_vals, d_gate], axis=3).astype(jnp.bfloat16).reshape(R * N, H * 4 * DH)
    d_norm = jnp.dot(d_proj, w_proj.T, preferred_element_type=jnp.float32).reshape(R, N, C)
    input_gradient = d_norm * layer_norm_gain
    pair_gradient = inverse_deviation * (input_gradient - lax.optimization_barrier(jnp.mean(input_gradient, axis=-1, keepdims=True)) - standardized_input * lax.optimization_barrier(jnp.mean(input_gradient * standardized_input, axis=-1, keepdims=True)))
    return (out, pair_gradient.astype(jnp.bfloat16))
```

```python
import functools

import jax
import jax.numpy as jnp
import numpy as np
from jax import lax
from jax.experimental import pallas as pl
from jax.experimental.pallas import tpu as pltpu
from jax.sharding import Mesh
from jax.sharding import PartitionSpec as P

DH = 32
SCALE = DH ** (-0.5)
EPS = 1e-05
NEG = -1e30
F32 = jnp.float32
BF16 = jnp.bfloat16
SWAP = [(0, 1), (1, 0)]


def vmem():
    return pl.BlockSpec(memory_space=pltpu.VMEM)


def smem():
    return pl.BlockSpec(memory_space=pltpu.SMEM)


def shapes(*items):
    return [jax.ShapeDtypeStruct(s, d) for s, d in items]


def call(kernel, outs, n_smem, n_vmem, scratch=(), flops=0, nbytes=0):
    return pl.pallas_call(
        kernel,
        out_shape=shapes(*outs),
        in_specs=[smem()] * n_smem + [vmem()] * n_vmem,
        out_specs=[vmem()] * len(outs),
        scratch_shapes=list(scratch),
        compiler_params=pltpu.CompilerParams(vmem_limit_bytes=48 * 1024 * 1024),
        cost_estimate=pl.CostEstimate(flops=flops, bytes_accessed=nbytes, transcendentals=0),
    )


def nt(a, b):
    return lax.dot_general(a, b, (((1,), (1,)), ((), ())), preferred_element_type=F32)


def nn(a, b):
    return jnp.dot(a, b, preferred_element_type=F32)


def bias_kernel(ids, bias, keep, send):
    xl = ids[1]
    for j in range(4):
        cols = pl.ds(j * 128, 128)
        keep[j] = bias[xl, :, cols].T
        send[j] = bias[1 - xl, :, cols].T


def norm(x):
    mean = jnp.mean(x, axis=-1, keepdims=True)
    centred = x - mean
    inv = lax.rsqrt(jnp.mean(centred * centred, axis=-1, keepdims=True) + EPS)
    return centred * inv, inv


def prep_kernel(ids, pair, gain, w_proj, w_out, d_out, keep, send, gate_out, go_out, proj_s):
    xl = ids[1]
    w_t = w_proj[...].T
    for p in range(2):
        for i in range(2):
            r = 2 * p + i
            xhat, _ = norm(pair[r].astype(F32))
            normed = (xhat * gain[...]).astype(BF16)
            proj = nt(w_t, normed)
            go = nt(w_out[...], d_out[r])
            go_out[r] = go
            for h in range(2):
                gate = jax.nn.sigmoid(proj[h * 128 + 96 : h * 128 + 128])
                gate_out[r, h * DH : (h + 1) * DH] = gate
                proj_s[h, i * 64 : (i + 1) * 64] = proj[h * 128 + 32 : h * 128 + 96]
                proj_s[h, 128 + i * 64 : 160 + i * 64] = proj[h * 128 : h * 128 + 32] * SCALE
                proj_s[h, 160 + i * 64 : 192 + i * 64] = go[h * DH : (h + 1) * DH] * gate
        for ref, h in ((keep, xl), (send, 1 - xl)):
            ref[p * 128 : (p + 1) * 128] = proj_s[h, 0:128].T.astype(BF16)
            ref[256 + p * 128 : 384 + p * 128] = proj_s[h, 128:256].astype(BF16)


def fill_queries(qd, packs):
    qd[...] = jnp.zeros_like(qd)
    for half, pack in enumerate(packs):
        for r in range(4):
            low = 64 * (r % 2)
            qd[half, r, low : low + 32, 0:128] = pack[256 + 64 * r : 288 + 64 * r]
            qd[half, r, low + 32 : low + 64, 128:256] = pack[288 + 64 * r : 320 + 64 * r]


def side(ids, which):
    xl = ids[1]
    return xl if which == 0 else 1 - xl


def tile_of(zk, xk):
    return zk // 2 + 8 * xk


def stats_kernel(ids, act, kv, bias, pack0, pack1, stats, qd, ms, ls, ds):
    fill_queries(qd, (pack0, pack1))
    z = ids[0]
    nz = kv.shape[0]
    for half in range(2):
        a = tile_of(z, side(ids, half))
        ms[...] = jnp.full_like(ms, NEG)
        ls[...] = jnp.zeros_like(ls)
        ds[...] = jnp.zeros_like(ds)
        for rel in range(2):
            xk = side(ids, rel)

            @pl.loop(0, nz)
            def _(zk):
                @pl.when(act[a, tile_of(zk, xk)] == 1)
                def _():
                    b = bias[zk // 4, xk, half, zk % 4].astype(F32)
                    for r in range(4):
                        sd = nn(kv[zk, rel, r // 2], qd[half, r])
                        s = (sd[:, :128] + b).reshape(16, 8, 128)
                        dp = sd[:, 128:].reshape(16, 8, 128)
                        m_old = ms[r]
                        m_new = jnp.maximum(m_old, jnp.max(s, axis=0))
                        e = jnp.exp(s - m_new[None])
                        c = jnp.exp(m_old - m_new)
                        ls[r] = ls[r] * c + jnp.sum(e, axis=0)
                        ds[r] = ds[r] * c + jnp.sum(e * dp, axis=0)
                        ms[r] = m_new

        for r in range(4):
            m = ms[r]
            top = jnp.max(m, axis=0, keepdims=True)
            f = jnp.exp(m - top)
            total = jnp.sum(ls[r] * f, axis=0, keepdims=True)
            stats[half, r, 0:1] = top + jnp.log(total)
            stats[half, r, 1:2] = jnp.sum(ds[r] * f, axis=0, keepdims=True) / total


def back_kernel(ids, act, kv, bias, pack0, pack1, stats, dkv, oq, qd, acc):
    fill_queries(qd, (pack0, pack1))
    oq[...] = jnp.zeros_like(oq)
    z = ids[0]
    nz = kv.shape[0]
    for rel in range(2):
        xk = side(ids, rel)

        @pl.loop(0, nz)
        def _(zk):
            acc[...] = jnp.zeros_like(acc)
            for half in range(2):
                a = tile_of(z, side(ids, half))

                @pl.when(act[a, tile_of(zk, xk)] == 1)
                def _():
                    b = bias[zk // 4, xk, half, zk % 4].astype(F32)
                    for p in range(2):
                        kvp = kv[zk, rel, p]
                        kvt = kvp.T
                        for i in range(2):
                            r = 2 * p + i
                            q = qd[half, r]
                            sd = nn(kvp, q)
                            prob = jnp.exp(sd[:, :128] + b - stats[half, r, 0:1])
                            dsc = prob * (sd[:, 128:] - stats[half, r, 1:2])
                            pd = jnp.concatenate([dsc.astype(BF16), prob.astype(BF16)], axis=1)
                            acc[p] += nt(pd, q)
                            t = nn(kvt[64 * i : 64 * i + 64], pd)
                            oq[half, r, 0:32] += t[0:32, 0:128]
                            oq[half, r, 32:64] += t[32:64, 128:256]

            for p in range(2):
                dkv[zk, rel, p] = acc[p].astype(BF16)

    for half in range(2):
        for r in range(4):
            oq[half, r, 0:32] *= SCALE


def out_kernel(ids, oq_own, oq_other, gate, w_out, keep, send):
    xl, c = ids[1], ids[2]
    w_t = w_out[...].T
    for r in range(4):
        mine, theirs = oq_own[0, r, 32:64], oq_other[r, 32:64].astype(F32)
        att = jnp.concatenate(
            [jnp.where(xl == 0, mine, theirs), jnp.where(xl == 0, theirs, mine)], axis=0
        )
        part = nn(w_t, (gate[r] * att).astype(BF16))
        low, high = part[0:64], part[64:128]
        keep[r] = jnp.where(c == 0, low, high)
        send[r] = jnp.where(c == 0, high, low).astype(BF16)


def proj_kernel(ids, oq_own, oq_other, dkv_own, dkv_other, gate, go, w_proj, keep, send, dp):
    xl = ids[1]
    for p in range(2):
        mine_kv, theirs_kv = dkv_own[p].astype(F32).T, dkv_other[p].astype(F32).T
        for i in range(2):
            r = 2 * p + i
            for oq, kvt, h in (
                (oq_own[0, r], mine_kv, xl),
                (oq_other[r].astype(F32), theirs_kv, 1 - xl),
            ):
                low = pl.multiple_of(h * DH, DH)
                g = gate[r, pl.ds(low, DH)]
                base = pl.multiple_of(h * 128, 128)
                dp[pl.ds(base, 32)] = oq[0:32]
                dp[pl.ds(base + 32, 64)] = kvt[64 * i : 64 * i + 64]
                dp[pl.ds(base + 96, 32)] = go[r, pl.ds(low, DH)] * oq[32:64] * g * (1.0 - g)
            part = nn(w_proj[...], dp[...].astype(BF16)).T
            keep[r] = part
            send[r] = part.astype(BF16)


def final_kernel(pair, gain, part, other, out):
    for r in range(4):
        xhat, inv = norm(pair[r].astype(F32))
        g = (part[r].astype(BF16).astype(F32) + other[r].astype(F32)) * gain[...]
        mean = jnp.mean(g, axis=-1, keepdims=True)
        along = jnp.mean(g * xhat, axis=-1, keepdims=True)
        out[r] = (inv * (g - mean - xhat * along)).astype(BF16)


def per_device(pair, gain, w_proj, w_out, tri_bias, active, d_out):
    z, xl, c = lax.axis_index("z"), lax.axis_index("xl"), lax.axis_index("c")
    ids = jnp.stack([z, xl, c, c]).astype(jnp.int32)
    gain = gain.reshape(1, 128)
    bias_keep, bias_send = call(bias_kernel, [((4, 128, 128), BF16)] * 2, 1, 1)(ids, tri_bias)
    bias = jnp.stack([bias_keep, lax.ppermute(bias_send, "xl", SWAP)])
    pack, pack_send, gate, go = call(
        prep_kernel,
        [((512, 128), BF16)] * 2 + [((4, 64, 128), F32)] * 2,
        1,
        5,
        [pltpu.VMEM((2, 256, 128), F32)],
    )(ids, pair, gain, w_proj, w_out, d_out)
    pack_other = lax.ppermute(pack_send, "xl", SWAP)
    kv = jnp.stack([pack[:256].reshape(2, 128, 128), pack_other[:256].reshape(2, 128, 128)])
    kv = lax.all_gather(kv, "z")
    bias = lax.all_gather(bias, "xh")
    bias = lax.all_gather(bias, "y")
    (stats,) = call(
        stats_kernel,
        [((2, 4, 2, 128), F32)],
        2,
        4,
        [pltpu.VMEM((2, 4, 128, 256), BF16)] + [pltpu.VMEM((4, 8, 128), F32)] * 3,
    )(ids, active, kv, bias, pack, pack_other)
    dkv, oq = call(
        back_kernel,
        [((16, 2, 2, 128, 128), BF16), ((2, 4, 64, 128), F32)],
        2,
        5,
        [pltpu.VMEM((2, 4, 128, 256), BF16), pltpu.VMEM((2, 128, 128), F32)],
    )(ids, active, kv, bias, pack, pack_other, stats)
    oq_other = lax.ppermute(oq[1].astype(BF16), "xl", SWAP)
    out_keep, out_send = call(
        out_kernel, [((4, 64, 128), F32), ((4, 64, 128), BF16)], 1, 4
    )(ids, oq, oq_other, gate, w_out)
    out = (out_keep + lax.ppermute(out_send, "c", SWAP).astype(F32)).astype(BF16)
    dkv = lax.psum_scatter(dkv, "z", scatter_dimension=0, tiled=False)
    dkv_other = lax.ppermute(dkv[1], "xl", SWAP)
    part, part_send = call(
        proj_kernel,
        [((4, 128, 128), F32), ((4, 128, 128), BF16)],
        1,
        7,
        [pltpu.VMEM((256, 128), F32)],
    )(ids, oq, oq_other, dkv[0], dkv_other, gate, go, w_proj)
    (pair_gradient,) = call(final_kernel, [((4, 128, 128), BF16)], 0, 4)(
        pair, gain, part, lax.ppermute(part_send, "c", SWAP)
    )
    return jnp.swapaxes(out, 1, 2), pair_gradient


def solution(mesh):
    fine = Mesh(np.asarray(mesh.devices).reshape(2, 4, 2, 16, 2), ("xh", "y", "xl", "z", "c"))
    row, col = ("xh", "y"), ("xl", "z")
    return jax.shard_map(
        per_device,
        mesh=fine,
        in_specs=(
            P(row, col, None),
            P(),
            P(None, "c"),
            P("c", None),
            P("c", col, row),
            P(),
            P(row, col, None),
        ),
        out_specs=(P(row, col, "c"), P(row, col, None)),
        check_vma=False,
    )
```

```python
import functools

import jax
import jax.numpy as jnp
import numpy as np
from jax import lax
from jax.experimental import pallas as pl
from jax.experimental.pallas import tpu as pltpu
from jax.sharding import Mesh
from jax.sharding import PartitionSpec as P

DH = 32
SCALE = DH ** (-0.5)
EPS = 1e-05
NEG = -1e30
F32 = jnp.float32
BF16 = jnp.bfloat16
SWAP = [(0, 1), (1, 0)]


def vmem():
    return pl.BlockSpec(memory_space=pltpu.VMEM)


def smem():
    return pl.BlockSpec(memory_space=pltpu.SMEM)


def shapes(*items):
    return [jax.ShapeDtypeStruct(s, d) for s, d in items]


def call(kernel, outs, n_smem, n_vmem, scratch=(), flops=0, nbytes=0):
    return pl.pallas_call(
        kernel,
        out_shape=shapes(*outs),
        in_specs=[smem()] * n_smem + [vmem()] * n_vmem,
        out_specs=[vmem()] * len(outs),
        scratch_shapes=list(scratch),
        compiler_params=pltpu.CompilerParams(vmem_limit_bytes=24 * 1024 * 1024),
        cost_estimate=pl.CostEstimate(flops=flops, bytes_accessed=nbytes, transcendentals=0),
    )


def nt(a, b):
    return lax.dot_general(a, b, (((1,), (1,)), ((), ())), preferred_element_type=F32)


def nn(a, b):
    return jnp.dot(a, b, preferred_element_type=F32)


def bias_kernel(ids, bias, keep, send):
    xl = ids[1]
    for j in range(4):
        cols = pl.ds(j * 128, 128)
        keep[j] = bias[xl, :, cols].T
        send[j] = bias[1 - xl, :, cols].T


def norm(x):
    mean = jnp.mean(x, axis=-1, keepdims=True)
    centred = x - mean
    inv = lax.rsqrt(jnp.mean(centred * centred, axis=-1, keepdims=True) + EPS)
    return centred * inv, inv


def prep_kernel(ids, pair, gain, w_proj, w_out, d_out, keep, send, gate_out, go_out, proj_s):
    xl = ids[1]
    w_t = w_proj[...].T
    for p in range(2):
        for i in range(2):
            r = 2 * p + i
            xhat, _ = norm(pair[r].astype(F32))
            normed = (xhat * gain[...]).astype(BF16)
            proj = nt(w_t, normed)
            go = nt(w_out[...], d_out[r])
            go_out[r] = go
            for h in range(2):
                gate = jax.nn.sigmoid(proj[h * 128 + 96 : h * 128 + 128])
                gate_out[r, h * DH : (h + 1) * DH] = gate
                proj_s[h, i * 64 : (i + 1) * 64] = proj[h * 128 + 32 : h * 128 + 96]
                proj_s[h, 128 + i * 64 : 160 + i * 64] = proj[h * 128 : h * 128 + 32] * SCALE
                proj_s[h, 160 + i * 64 : 192 + i * 64] = go[h * DH : (h + 1) * DH] * gate
        for ref, h in ((keep, xl), (send, 1 - xl)):
            ref[p * 128 : (p + 1) * 128] = proj_s[h, 0:128].T.astype(BF16)
            ref[256 + p * 128 : 384 + p * 128] = proj_s[h, 128:256].astype(BF16)


def fill_queries(qd, packs):
    qd[...] = jnp.zeros_like(qd)
    for half, pack in enumerate(packs):
        for r in range(4):
            low = 64 * (r % 2)
            qd[half, r, low : low + 32, 0:128] = pack[256 + 64 * r : 288 + 64 * r]
            qd[half, r, low + 32 : low + 64, 128:256] = pack[288 + 64 * r : 320 + 64 * r]


def tile_of(zk, xk):
    return zk // 2 + 8 * xk


def list_units(ids, act, lst, a, first, count):
    def step(u, n):
        zk = (ids[0] + first + 4 * (u // 2) + 32) % 16
        xk = jnp.where(u % 2 == 0, ids[1], 1 - ids[1])
        lst[n] = u
        return n + act[a, tile_of(zk, xk)]

    return lax.fori_loop(0, 2 * count, step, 0)


def load_units(ids, kv, bias, first, half, units):
    keys = [[kv[u // 2, u % 2, p] for u in units] for p in range(2)]
    b = []
    for u in units:
        zk = (ids[0] + first + 4 * (u // 2) + 32) % 16
        xk = jnp.where(u % 2 == 0, ids[1], 1 - ids[1])
        b.append(bias[zk // 4, jnp.where(xk == ids[3], 0, 1), half, zk % 4].astype(F32))
    keys = [k[0] if len(k) == 1 else jnp.concatenate(k, axis=0) for k in keys]
    return keys, b[0] if len(b) == 1 else jnp.concatenate(b, axis=0)


def over_units(ids, act, lst, first, count, half, body):
    a = tile_of(ids[0], jnp.where(half == 0, ids[1], 1 - ids[1]))
    n = list_units(ids, act, lst, a, first, count)

    @pl.loop(0, n // 2)
    def _(k):
        body([lst[2 * k], lst[2 * k + 1]])

    @pl.when(n % 2 == 1)
    def _():
        body([lst[n - 1]])


def stats_kernel(firsts, begin, end, ids, act, *refs):
    n = len(firsts)
    kvs, (bias, pack0, pack1), refs = refs[:n], refs[n : n + 3], refs[n + 3 :]
    before, refs = (None, refs) if begin else (refs[0], refs[1:])
    out, qd, lst, st = refs
    fill_queries(qd, (pack0, pack1))
    if begin:
        st[0] = jnp.full(st.shape[1:], NEG, F32)
        st[1:3] = jnp.zeros((2,) + st.shape[1:], F32)
    else:
        st[...] = before[...]

    @pl.loop(0, 2)
    def _(half):
        for kv, first in zip(kvs, firsts):

            def body(units, kv=kv, first=first):
                keys, b = load_units(ids, kv, bias, first, half, units)
                rows = b.shape[0] // 8
                for p in range(2):
                    sd = [nn(keys[p], qd[half, 2 * p + i]) for i in range(2)]
                    for i in range(2):
                        r = 2 * p + i
                        s = (sd[i][:, :128] + b).reshape(rows, 8, 128)
                        dp = sd[i][:, 128:].reshape(rows, 8, 128)
                        m_old = st[0, half, r]
                        m_new = jnp.maximum(m_old, jnp.max(s, axis=0))
                        e = jnp.exp(s - m_new[None])
                        c = jnp.exp(m_old - m_new)
                        st[1, half, r] = st[1, half, r] * c + jnp.sum(e, axis=0)
                        st[2, half, r] = st[2, half, r] * c + jnp.sum(e * dp, axis=0)
                        st[0, half, r] = m_new

            over_units(ids, act, lst, first, kv.shape[0], half, body)

    if not end:
        out[...] = st[...]
        return
    for half in range(2):
        for r in range(4):
            m = st[0, half, r]
            top = jnp.max(m, axis=0, keepdims=True)
            f = jnp.exp(m - top)
            total = jnp.sum(st[1, half, r] * f, axis=0, keepdims=True)
            out[half, r, 0:1] = top + jnp.log(total)
            out[half, r, 1:2] = jnp.sum(st[2, half, r] * f, axis=0, keepdims=True) / total


def back_kernel(firsts, ids, act, *refs):
    n = len(firsts)
    kvs, (bias, pack0, pack1, stats) = refs[:n], refs[n : n + 4]
    dkvs, (oq, qd, lst, acc) = refs[n + 4 : 2 * n + 4], refs[2 * n + 4 :]
    fill_queries(qd, (pack0, pack1))
    oq[...] = jnp.zeros_like(oq)
    for kv, dkv, first in zip(kvs, dkvs, firsts):
        count = kv.shape[0]
        acc[0:count] = jnp.zeros((count,) + acc.shape[1:], F32)

        @pl.loop(0, 2)
        def _(half):
            def body(units):
                keys, b = load_units(ids, kv, bias, first, half, units)
                for p in range(2):
                    keys_t = keys[p].T
                    qs = [qd[half, 2 * p + i] for i in range(2)]
                    sd = [nn(keys[p], q) for q in qs]
                    pds = []
                    for i in range(2):
                        r = 2 * p + i
                        prob = jnp.exp(sd[i][:, :128] + (b - stats[half, r, 0:1]))
                        dsc = prob * (sd[i][:, 128:] - stats[half, r, 1:2])
                        pds.append(jnp.concatenate([dsc.astype(BF16), prob.astype(BF16)], axis=1))
                    both = nt(jnp.concatenate(pds, axis=1), jnp.concatenate(qs, axis=1))
                    for k, u in enumerate(units):
                        acc[u // 2, u % 2, p] += both[128 * k : 128 * k + 128]
                    for i in range(2):
                        r = 2 * p + i
                        t = nn(keys_t[64 * i : 64 * i + 64], pds[i])
                        oq[half, r, 0:32] += t[0:32, 0:128]
                        oq[half, r, 32:64] += t[32:64, 128:256]

            over_units(ids, act, lst, first, count, half, body)

        dkv[...] = acc[0:count].astype(BF16)


def out_kernel(ids, oq_own, oq_other, gate, w_out, keep, send):
    xl, c = ids[1], ids[2]
    w_t = w_out[...].T
    for r in range(4):
        mine, theirs = oq_own[0, r, 32:64], oq_other[r, 32:64].astype(F32)
        att = jnp.concatenate(
            [jnp.where(xl == 0, mine, theirs), jnp.where(xl == 0, theirs, mine)], axis=0
        )
        part = nn(w_t, (gate[r] * att).astype(BF16))
        low, high = part[0:64], part[64:128]
        keep[r] = jnp.where(c == 0, low, high)
        send[r] = jnp.where(c == 0, high, low).astype(BF16)


def proj_kernel(ids, oq_own, oq_other, dkv_own, dkv_other, gate, go, w_proj, keep, send, dp):
    xl = ids[1]
    for p in range(2):
        mine_kv, theirs_kv = dkv_own[p].astype(F32).T, dkv_other[p].astype(F32).T
        for i in range(2):
            r = 2 * p + i
            for oq, kvt, h in (
                (oq_own[0, r], mine_kv, xl),
                (oq_other[r].astype(F32), theirs_kv, 1 - xl),
            ):
                low = pl.multiple_of(h * DH, DH)
                g = gate[r, pl.ds(low, DH)]
                base = pl.multiple_of(h * 128, 128)
                dp[pl.ds(base, 32)] = oq[0:32]
                dp[pl.ds(base + 32, 64)] = kvt[64 * i : 64 * i + 64]
                dp[pl.ds(base + 96, 32)] = go[r, pl.ds(low, DH)] * oq[32:64] * g * (1.0 - g)
            part = nn(w_proj[...], dp[...].astype(BF16)).T
            keep[r] = part
            send[r] = part.astype(BF16)


def final_kernel(pair, gain, part, other, out):
    for r in range(4):
        xhat, inv = norm(pair[r].astype(F32))
        g = (part[r].astype(BF16).astype(F32) + other[r].astype(F32)) * gain[...]
        mean = jnp.mean(g, axis=-1, keepdims=True)
        along = jnp.mean(g * xhat, axis=-1, keepdims=True)
        out[r] = (inv * (g - mean - xhat * along)).astype(BF16)


def stats_call(firsts, begin, end, ids, active, kvs, rest):
    out = ((2, 4, 2, 128), F32) if end else ((3, 2, 4, 8, 128), F32)
    return call(
        functools.partial(stats_kernel, firsts, begin, end),
        [out],
        2,
        len(kvs) + len(rest),
        [
            pltpu.VMEM((2, 4, 128, 256), BF16),
            pltpu.SMEM((9,), jnp.int32),
            pltpu.VMEM((3, 2, 4, 8, 128), F32),
        ],
        flops=10 ** 9,
        nbytes=10 ** 7,
    )(ids, active, *kvs, *rest)[0]


def back_call(firsts, ids, active, kvs, rest):
    res = call(
        functools.partial(back_kernel, firsts),
        [(kv.shape, BF16) for kv in kvs] + [((2, 4, 64, 128), F32)],
        2,
        len(kvs) + len(rest),
        [
            pltpu.VMEM((2, 4, 128, 256), BF16),
            pltpu.SMEM((9,), jnp.int32),
            pltpu.VMEM((4, 2, 2, 128, 128), F32),
        ],
        flops=2 * 10 ** 9,
        nbytes=2 * 10 ** 7,
    )(ids, active, *kvs, *rest)
    return res[:-1], res[-1]


def to_z(x, step):
    return lax.ppermute(x, "z", [(j, (j + step) % 16) for j in range(16)])


def per_device(pair, gain, w_proj, w_out, tri_bias, active, d_out):
    z, xl, c, xh = (lax.axis_index(name) for name in ("z", "xl", "c", "xh"))
    ids = jnp.stack([z, xl, c, xh]).astype(jnp.int32)
    gain = gain.reshape(1, 128)
    pack, pack_send, gate, go = call(
        prep_kernel,
        [((512, 128), BF16)] * 2 + [((4, 64, 128), F32)] * 2,
        1,
        5,
        [pltpu.VMEM((2, 256, 128), F32)],
    )(ids, pair, gain, w_proj, w_out, d_out)
    pack_other = lax.ppermute(pack_send, "xl", SWAP)
    bias_keep, bias_send = call(bias_kernel, [((4, 128, 128), BF16)] * 2, 1, 1)(ids, tri_bias)
    bias = jnp.stack([bias_keep, lax.ppermute(bias_send, "xl", SWAP)])
    bias = jnp.stack([bias, lax.ppermute(bias, "xh", SWAP)])
    bias = lax.all_gather(bias, "y")
    kv = jnp.stack([pack[:256].reshape(2, 128, 128), pack_other[:256].reshape(2, 128, 128)])
    own = jnp.stack([to_z(kv, 4), kv, to_z(kv, -4), to_z(kv, 8)])
    up, down = to_z(own, -1), to_z(own, 1)
    up2, down2 = to_z(own[1:3], -2), to_z(own[0:2], 2)
    rest = (bias, pack, pack_other)
    state = stats_call((-4,), True, False, ids, active, (own,), rest)
    state = stats_call((-3, -5), False, False, ids, active, (up, down), rest + (state,))
    stats = stats_call((2, -6), False, True, ids, active, (up2, down2), rest + (state,))
    rest = rest + (stats,)
    (d_up2, d_down2), oq2 = back_call((2, -6), ids, active, (up2, down2), rest)
    r_up2, r_down2 = to_z(d_up2, 2), to_z(d_down2, -2)
    (d_up,), oq1 = back_call((-3,), ids, active, (up,), rest)
    r_up = to_z(d_up, 1)
    (d_down,), oq3 = back_call((-5,), ids, active, (down,), rest)
    r_down = to_z(d_down, -1)
    (d_own,), oq0 = back_call((-4,), ids, active, (own,), rest)
    oq = oq0 + oq1 + oq2 + oq3
    oq = jnp.concatenate([oq[:, :, :32] * SCALE, oq[:, :, 32:]], axis=2)
    oq_other = lax.ppermute(oq[1].astype(BF16), "xl", SWAP)
    out_keep, out_send = call(
        out_kernel, [((4, 64, 128), F32), ((4, 64, 128), BF16)], 1, 4
    )(ids, oq, oq_other, gate, w_out)
    out = (out_keep + lax.ppermute(out_send, "c", SWAP).astype(F32)).astype(BF16)
    f = lambda x: x.astype(F32)
    sums = f(d_own) + f(r_up) + f(r_down)
    s0 = (sums[0] + f(r_down2[0])).astype(BF16)
    s1 = sums[1] + f(r_up2[0]) + f(r_down2[1])
    s2 = (sums[2] + f(r_up2[1])).astype(BF16)
    s3 = sums[3].astype(BF16)
    dkv = s1 + f(to_z(s0, -4)) + f(to_z(s2, 4)) + f(to_z(s3, 8))
    dkv_other = lax.ppermute(dkv[1].astype(BF16), "xl", SWAP)
    part, part_send = call(
        proj_kernel,
        [((4, 128, 128), F32), ((4, 128, 128), BF16)],
        1,
        7,
        [pltpu.VMEM((256, 128), F32)],
    )(ids, oq, oq_other, dkv[0], dkv_other, gate, go, w_proj)
    (pair_gradient,) = call(final_kernel, [((4, 128, 128), BF16)], 0, 4)(
        pair, gain, part, lax.ppermute(part_send, "c", SWAP)
    )
    return jnp.swapaxes(out, 1, 2), pair_gradient


def solution(mesh):
    fine = Mesh(np.asarray(mesh.devices).reshape(2, 4, 2, 16, 2), ("xh", "y", "xl", "z", "c"))
    row, col = ("xh", "y"), ("xl", "z")
    return jax.shard_map(
        per_device,
        mesh=fine,
        in_specs=(
            P(row, col, None),
            P(),
            P(None, "c"),
            P("c", None),
            P("c", col, row),
            P(),
            P(row, col, None),
        ),
        out_specs=(P(row, col, "c"), P(row, col, None)),
        check_vma=False,
    )
```

```python
import functools

import jax
import jax.numpy as jnp
import numpy as np
from jax import lax
from jax.experimental import pallas as pl
from jax.experimental.pallas import tpu as pltpu
from jax.sharding import Mesh
from jax.sharding import PartitionSpec as P

DH = 32
SCALE = DH ** (-0.5)
EPS = 1e-05
NEG = -1e30
F32 = jnp.float32
BF16 = jnp.bfloat16
SWAP = [(0, 1), (1, 0)]


def vmem():
    return pl.BlockSpec(memory_space=pltpu.VMEM)


def smem():
    return pl.BlockSpec(memory_space=pltpu.SMEM)


def shapes(*items):
    return [jax.ShapeDtypeStruct(s, d) for s, d in items]


def call(kernel, outs, n_smem, n_vmem, scratch=(), flops=0, nbytes=0):
    return pl.pallas_call(
        kernel,
        out_shape=shapes(*outs),
        in_specs=[smem()] * n_smem + [vmem()] * n_vmem,
        out_specs=[vmem()] * len(outs),
        scratch_shapes=list(scratch),
        compiler_params=pltpu.CompilerParams(vmem_limit_bytes=24 * 1024 * 1024),
        cost_estimate=pl.CostEstimate(flops=flops, bytes_accessed=nbytes, transcendentals=0),
    )


def nt(a, b):
    return lax.dot_general(a, b, (((1,), (1,)), ((), ())), preferred_element_type=F32)


def nn(a, b):
    return jnp.dot(a, b, preferred_element_type=F32)


def bias_kernel(bias, send):
    for j in range(4):
        for h in range(2):
            block = bias[h, :, 128 * j : 128 * j + 128].T
            send[h, j] = block
            send[2 + h, j] = block


def norm(x):
    mean = jnp.mean(x, axis=-1, keepdims=True)
    centred = x - mean
    inv = lax.rsqrt(jnp.mean(centred * centred, axis=-1, keepdims=True) + EPS)
    return centred * inv, inv


def prep_kernel(ids, pair, gain, w_proj, w_out, d_out, keep, send, gate_out, go_out, proj_s):
    xl = ids[1]
    w_t = w_proj[...].T
    for p in range(2):
        for i in range(2):
            r = 2 * p + i
            xhat, _ = norm(pair[r].astype(F32))
            normed = (xhat * gain[...]).astype(BF16)
            proj = nt(w_t, normed)
            go = nt(w_out[...], d_out[r])
            go_out[r] = go
            for h in range(2):
                gate = jax.nn.sigmoid(proj[h * 128 + 96 : h * 128 + 128])
                gate_out[r, h * DH : (h + 1) * DH] = gate
                proj_s[h, i * 64 : (i + 1) * 64] = proj[h * 128 + 32 : h * 128 + 96]
                proj_s[h, 128 + i * 64 : 160 + i * 64] = proj[h * 128 : h * 128 + 32] * SCALE
                proj_s[h, 160 + i * 64 : 192 + i * 64] = go[h * DH : (h + 1) * DH] * gate
        for ref, h in ((keep, xl), (send, 1 - xl)):
            ref[p * 128 : (p + 1) * 128] = proj_s[h, 0:128].T.astype(BF16)
            ref[256 + p * 128 : 384 + p * 128] = proj_s[h, 128:256].astype(BF16)


def fill_queries(qd, packs):
    qd[...] = jnp.zeros_like(qd)
    for half, pack in enumerate(packs):
        for r in range(4):
            low = 64 * (r % 2)
            qd[half, r, low : low + 32, 0:128] = pack[256 + 64 * r : 288 + 64 * r]
            qd[half, r, low + 32 : low + 64, 128:256] = pack[288 + 64 * r : 320 + 64 * r]


def tile_of(zk, xk):
    return zk // 2 + 8 * xk


def list_units(ids, act, lst, a, first, count):
    def step(u, n):
        zk = (ids[0] + first + 4 * (u // 2) + 32) % 16
        xk = jnp.where(u % 2 == 0, ids[1], 1 - ids[1])
        lst[n] = u
        return n + act[a, tile_of(zk, xk)]

    return lax.fori_loop(0, 2 * count, step, 0)


def load_units(ids, kv, bias, first, half, units):
    keys = [[kv[u // 2, u % 2, p] for u in units] for p in range(2)]
    b = []
    for u in units:
        zk = (ids[0] + first + 4 * (u // 2) + 32) % 16
        xk = jnp.where(u % 2 == 0, ids[1], 1 - ids[1])
        b.append(bias[zk // 4, xk, jnp.where(half == 0, ids[1], 1 - ids[1]), zk % 4].astype(F32))
    keys = [k[0] if len(k) == 1 else jnp.concatenate(k, axis=0) for k in keys]
    return keys, b[0] if len(b) == 1 else jnp.concatenate(b, axis=0)


def over_units(ids, act, lst, first, count, half, body):
    a = tile_of(ids[0], jnp.where(half == 0, ids[1], 1 - ids[1]))
    n = list_units(ids, act, lst, a, first, count)

    @pl.loop(0, n // 2)
    def _(k):
        body([lst[2 * k], lst[2 * k + 1]])

    @pl.when(n % 2 == 1)
    def _():
        body([lst[n - 1]])


def stats_kernel(firsts, begin, end, ids, act, *refs):
    n = len(firsts)
    kvs, (bias, pack0, pack1), refs = refs[:n], refs[n : n + 3], refs[n + 3 :]
    before, refs = (None, refs) if begin else (refs[0], refs[1:])
    out, qd, lst, st = refs
    fill_queries(qd, (pack0, pack1))
    if begin:
        st[0] = jnp.full(st.shape[1:], NEG, F32)
        st[1:3] = jnp.zeros((2,) + st.shape[1:], F32)
    else:
        st[...] = before[...]

    @pl.loop(0, 2)
    def _(half):
        for kv, first in zip(kvs, firsts):

            def body(units, kv=kv, first=first):
                keys, b = load_units(ids, kv, bias, first, half, units)
                rows = b.shape[0] // 8
                for p in range(2):
                    sd = [nn(keys[p], qd[half, 2 * p + i]) for i in range(2)]
                    for i in range(2):
                        r = 2 * p + i
                        s = (sd[i][:, :128] + b).reshape(rows, 8, 128)
                        dp = sd[i][:, 128:].reshape(rows, 8, 128)
                        m_old = st[0, half, r]
                        m_new = jnp.maximum(m_old, jnp.max(s, axis=0))
                        e = jnp.exp(s - m_new[None])
                        c = jnp.exp(m_old - m_new)
                        st[1, half, r] = st[1, half, r] * c + jnp.sum(e, axis=0)
                        st[2, half, r] = st[2, half, r] * c + jnp.sum(e * dp, axis=0)
                        st[0, half, r] = m_new

            over_units(ids, act, lst, first, kv.shape[0], half, body)

    if not end:
        out[...] = st[...]
        return
    for half in range(2):
        for r in range(4):
            m = st[0, half, r]
            top = jnp.max(m, axis=0, keepdims=True)
            f = jnp.exp(m - top)
            total = jnp.sum(st[1, half, r] * f, axis=0, keepdims=True)
            out[half, r, 0:1] = top + jnp.log(total)
            out[half, r, 1:2] = jnp.sum(st[2, half, r] * f, axis=0, keepdims=True) / total


def back_kernel(firsts, ids, act, *refs):
    n = len(firsts)
    kvs, (bias, pack0, pack1, stats) = refs[:n], refs[n : n + 4]
    dkvs, (oq, qd, lst, acc) = refs[n + 4 : 2 * n + 4], refs[2 * n + 4 :]
    fill_queries(qd, (pack0, pack1))
    oq[...] = jnp.zeros_like(oq)
    for kv, dkv, first in zip(kvs, dkvs, firsts):
        count = kv.shape[0]
        acc[0:count] = jnp.zeros((count,) + acc.shape[1:], F32)

        @pl.loop(0, 2)
        def _(half):
            def body(units):
                keys, b = load_units(ids, kv, bias, first, half, units)
                for p in range(2):
                    keys_t = keys[p].T
                    qs = [qd[half, 2 * p + i] for i in range(2)]
                    sd = [nn(keys[p], q) for q in qs]
                    pds = []
                    for i in range(2):
                        r = 2 * p + i
                        prob = jnp.exp(sd[i][:, :128] + (b - stats[half, r, 0:1]))
                        dsc = prob * (sd[i][:, 128:] - stats[half, r, 1:2])
                        pds.append(jnp.concatenate([dsc.astype(BF16), prob.astype(BF16)], axis=1))
                    both = nt(jnp.concatenate(pds, axis=1), jnp.concatenate(qs, axis=1))
                    for k, u in enumerate(units):
                        acc[u // 2, u % 2, p] += both[128 * k : 128 * k + 128]
                    for i in range(2):
                        r = 2 * p + i
                        t = nn(keys_t[64 * i : 64 * i + 64], pds[i])
                        oq[half, r, 0:32] += t[0:32, 0:128]
                        oq[half, r, 32:64] += t[32:64, 128:256]

            over_units(ids, act, lst, first, count, half, body)

        dkv[...] = acc[0:count].astype(BF16)


def out_kernel(ids, oq_own, oq_other, gate, w_out, keep, send):
    xl, c = ids[1], ids[2]
    w_t = w_out[...].T
    for r in range(4):
        mine, theirs = oq_own[0, r, 32:64], oq_other[r, 32:64].astype(F32)
        att = jnp.concatenate(
            [jnp.where(xl == 0, mine, theirs), jnp.where(xl == 0, theirs, mine)], axis=0
        )
        part = nn(w_t, (gate[r] * att).astype(BF16))
        low, high = part[0:64], part[64:128]
        keep[r] = jnp.where(c == 0, low, high)
        send[r] = jnp.where(c == 0, high, low).astype(BF16)


def sum_kernel(ids, d_own, r_up, r_down, r_up2, r_down2, out):
    m = ids[0] // 4
    for e in range(4):
        total = d_own[e].astype(F32) + r_up[e].astype(F32) + r_down[e].astype(F32)
        if e in (1, 2):
            total += r_up2[e - 1].astype(F32)
        if e in (0, 1):
            total += r_down2[e].astype(F32)
        out[(m + e + 3) % 4] = total.astype(BF16)


def proj_kernel(ids, oq_own, oq_other, dkv_own, dkv_other, gate, go, w_proj, keep, send, dp):
    xl = ids[1]
    for p in range(2):
        mine_kv = sum(dkv_own[m, 0, p].astype(F32) for m in range(4)).T
        theirs_kv = dkv_other[p].astype(F32).T
        for i in range(2):
            r = 2 * p + i
            for oq, kvt, h in (
                (oq_own[0, r], mine_kv, xl),
                (oq_other[r].astype(F32), theirs_kv, 1 - xl),
            ):
                low = pl.multiple_of(h * DH, DH)
                g = gate[r, pl.ds(low, DH)]
                base = pl.multiple_of(h * 128, 128)
                dp[pl.ds(base, 32)] = oq[0:32]
                dp[pl.ds(base + 32, 64)] = kvt[64 * i : 64 * i + 64]
                dp[pl.ds(base + 96, 32)] = go[r, pl.ds(low, DH)] * oq[32:64] * g * (1.0 - g)
            part = nn(w_proj[...], dp[...].astype(BF16)).T
            keep[r] = part
            send[r] = part.astype(BF16)


def final_kernel(pair, gain, part, other, out):
    for r in range(4):
        xhat, inv = norm(pair[r].astype(F32))
        g = (part[r].astype(BF16).astype(F32) + other[r].astype(F32)) * gain[...]
        mean = jnp.mean(g, axis=-1, keepdims=True)
        along = jnp.mean(g * xhat, axis=-1, keepdims=True)
        out[r] = (inv * (g - mean - xhat * along)).astype(BF16)


def stats_call(firsts, begin, end, ids, active, kvs, rest):
    out = ((2, 4, 2, 128), F32) if end else ((3, 2, 4, 8, 128), F32)
    return call(
        functools.partial(stats_kernel, firsts, begin, end),
        [out],
        2,
        len(kvs) + len(rest),
        [
            pltpu.VMEM((2, 4, 128, 256), BF16),
            pltpu.SMEM((9,), jnp.int32),
            pltpu.VMEM((3, 2, 4, 8, 128), F32),
        ],
        flops=10 ** 9,
        nbytes=10 ** 7,
    )(ids, active, *kvs, *rest)[0]


def back_call(firsts, ids, active, kvs, rest):
    res = call(
        functools.partial(back_kernel, firsts),
        [(kv.shape, BF16) for kv in kvs] + [((2, 4, 64, 128), F32)],
        2,
        len(kvs) + len(rest),
        [
            pltpu.VMEM((2, 4, 128, 256), BF16),
            pltpu.SMEM((9,), jnp.int32),
            pltpu.VMEM((4, 2, 2, 128, 128), F32),
        ],
        flops=2 * 10 ** 9,
        nbytes=2 * 10 ** 7,
    )(ids, active, *kvs, *rest)
    return res[:-1], res[-1]


def to_z(x, step):
    return lax.ppermute(x, "z", [(j, (j + step) % 16) for j in range(16)])


def per_device(pair, gain, w_proj, w_out, tri_bias, active, d_out):
    ids = jnp.stack([lax.axis_index(name) for name in ("z", "xl", "c")]).astype(jnp.int32)
    gain = gain.reshape(1, 128)
    pack, pack_send, gate, go = call(
        prep_kernel,
        [((512, 128), BF16)] * 2 + [((4, 64, 128), F32)] * 2,
        1,
        5,
        [pltpu.VMEM((2, 256, 128), F32)],
    )(ids, pair, gain, w_proj, w_out, d_out)
    pack_other = lax.ppermute(pack_send, "xl", SWAP)
    tri_bias, _ = lax.optimization_barrier((tri_bias, pack_send))
    (bias,) = call(bias_kernel, [((4, 4, 128, 128), BF16)], 0, 1)(tri_bias)
    bias = lax.all_to_all(bias, ("xh", "xl"), 0, 0, tiled=True).reshape(2, 2, 4, 128, 128)
    bias, pack_other = lax.optimization_barrier((bias, pack_other))
    bias = lax.all_gather(bias, "y")
    kv = jnp.stack([pack[:256].reshape(2, 128, 128), pack_other[:256].reshape(2, 128, 128)])
    own = jnp.stack([to_z(kv, 4), kv, to_z(kv, -4), to_z(kv, 8)])
    up, down = to_z(own, -1), to_z(own, 1)
    up2, down2 = to_z(own[1:3], -2), to_z(own[0:2], 2)
    rest = (bias, pack, pack_other)
    state = stats_call((-4,), True, False, ids, active, (own,), rest)
    state = stats_call((-3, -5), False, False, ids, active, (up, down), rest + (state,))
    stats = stats_call((2, -6), False, True, ids, active, (up2, down2), rest + (state,))
    (d_up,), oq1 = back_call((-3,), ids, active, (up,), rest + (stats,))
    r_up = to_z(d_up, 1)
    (d_down,), oq3 = back_call((-5,), ids, active, (down,), rest + (stats,))
    r_down = to_z(d_down, -1)
    (d_up2, d_down2), oq2 = back_call((2, -6), ids, active, (up2, down2), rest + (stats,))
    r_up2, r_down2 = to_z(d_up2, 2), to_z(d_down2, -2)
    (d_own,), oq0 = back_call((-4,), ids, active, (own,), rest + (stats,))
    oq = oq0 + oq1 + oq2 + oq3
    oq = jnp.concatenate([oq[:, :, :32] * SCALE, oq[:, :, 32:]], axis=2)
    oq_other = lax.ppermute(oq[1].astype(BF16), "xl", SWAP)
    out_keep, out_send = call(
        out_kernel, [((4, 64, 128), F32), ((4, 64, 128), BF16)], 1, 4
    )(ids, oq, oq_other, gate, w_out)
    out = (out_keep + lax.ppermute(out_send, "c", SWAP).astype(F32)).astype(BF16)
    (sums,) = call(sum_kernel, [((4, 2, 2, 128, 128), BF16)], 1, 5)(
        ids, d_own, r_up, r_down, r_up2, r_down2
    )
    groups = [[k + 4 * m for m in range(4)] for k in range(4)]
    dkv = lax.all_to_all(sums, "z", 0, 0, axis_index_groups=groups, tiled=True)
    theirs = jnp.sum(dkv[:, 1].astype(F32), axis=0).astype(BF16)
    dkv_other = lax.ppermute(theirs, "xl", SWAP)
    part, part_send = call(
        proj_kernel,
        [((4, 128, 128), F32), ((4, 128, 128), BF16)],
        1,
        7,
        [pltpu.VMEM((256, 128), F32)],
    )(ids, oq, oq_other, dkv, dkv_other, gate, go, w_proj)
    (pair_gradient,) = call(final_kernel, [((4, 128, 128), BF16)], 0, 4)(
        pair, gain, part, lax.ppermute(part_send, "c", SWAP)
    )
    return jnp.swapaxes(out, 1, 2), pair_gradient


def solution(mesh):
    fine = Mesh(np.asarray(mesh.devices).reshape(2, 4, 2, 16, 2), ("xh", "y", "xl", "z", "c"))
    row, col = ("xh", "y"), ("xl", "z")
    return jax.shard_map(
        per_device,
        mesh=fine,
        in_specs=(
            P(row, col, None),
            P(),
            P(None, "c"),
            P("c", None),
            P("c", col, row),
            P(),
            P(row, col, None),
        ),
        out_specs=(P(row, col, "c"), P(row, col, None)),
        check_vma=False,
    )
```

```python
import functools

import jax
import jax.numpy as jnp
import numpy as np
from jax import lax
from jax.experimental import pallas as pl
from jax.experimental.pallas import tpu as pltpu
from jax.sharding import Mesh
from jax.sharding import PartitionSpec as P

DH = 32
SCALE = DH ** (-0.5)
EPS = 1e-05
NEG = -1e30
F32 = jnp.float32
BF16 = jnp.bfloat16
SWAP = [(0, 1), (1, 0)]


def vmem():
    return pl.BlockSpec(memory_space=pltpu.VMEM)


def smem():
    return pl.BlockSpec(memory_space=pltpu.SMEM)


def shapes(*items):
    return [jax.ShapeDtypeStruct(s, d) for s, d in items]


def call(kernel, outs, n_smem, n_vmem, scratch=(), flops=0, nbytes=0):
    return pl.pallas_call(
        kernel,
        out_shape=shapes(*outs),
        in_specs=[smem()] * n_smem + [vmem()] * n_vmem,
        out_specs=[vmem()] * len(outs),
        scratch_shapes=list(scratch),
        compiler_params=pltpu.CompilerParams(vmem_limit_bytes=24 * 1024 * 1024),
        cost_estimate=pl.CostEstimate(flops=flops, bytes_accessed=nbytes, transcendentals=0),
    )


def nt(a, b):
    return lax.dot_general(a, b, (((1,), (1,)), ((), ())), preferred_element_type=F32)


def nn(a, b):
    return jnp.dot(a, b, preferred_element_type=F32)


def norm(x):
    mean = jnp.mean(x, axis=-1, keepdims=True)
    centred = x - mean
    inv = lax.rsqrt(jnp.mean(centred * centred, axis=-1, keepdims=True) + EPS)
    return centred * inv, inv


def prep_kernel(ids, *refs):
    here, (keep, send, gate_out, go_out, bias_out) = refs[:6], refs[6:11]
    pair, gain, w_proj, w_out, d_out, bias = local = refs[11:17]
    proj_s, sems = refs[17:]
    copies = [pltpu.make_async_copy(s, d, sems.at[k]) for k, (s, d) in enumerate(zip(here, local))]
    for copy in copies:
        copy.start()
    for copy in copies[:5]:
        copy.wait()
    xl = ids[1]
    w_t = w_proj[...].T
    for p in range(2):
        for i in range(2):
            r = 2 * p + i
            xhat, _ = norm(pair[r].astype(F32))
            normed = (xhat * gain[...]).astype(BF16)
            proj = nt(w_t, normed)
            go = nt(w_out[...], d_out[r])
            go_out[r] = go
            for h in range(2):
                gate = jax.nn.sigmoid(proj[h * 128 + 96 : h * 128 + 128])
                gate_out[r, h * DH : (h + 1) * DH] = gate
                proj_s[h, i * 64 : (i + 1) * 64] = proj[h * 128 + 32 : h * 128 + 96]
                proj_s[h, 128 + i * 64 : 160 + i * 64] = proj[h * 128 : h * 128 + 32] * SCALE
                proj_s[h, 160 + i * 64 : 192 + i * 64] = go[h * DH : (h + 1) * DH] * gate
        for ref, h in ((keep, xl), (send, 1 - xl)):
            ref[p * 128 : (p + 1) * 128] = proj_s[h, 0:128].T.astype(BF16)
            ref[256 + p * 128 : 384 + p * 128] = proj_s[h, 128:256].astype(BF16)
    copies[5].wait()
    for j in range(4):
        for h in range(2):
            block = bias[h, :, 128 * j : 128 * j + 128].T
            bias_out[h, j] = block
            bias_out[2 + h, j] = block


def fill_queries(qd, packs):
    qd[...] = jnp.zeros_like(qd)
    for half, pack in enumerate(packs):
        for r in range(4):
            low = 64 * (r % 2)
            qd[half, r, low : low + 32, 0:128] = pack[256 + 64 * r : 288 + 64 * r]
            qd[half, r, low + 32 : low + 64, 128:256] = pack[288 + 64 * r : 320 + 64 * r]


def tile_of(zk, xk):
    return zk // 2 + 8 * xk


def list_units(ids, act, lst, a, first, count):
    def step(u, n):
        zk = (ids[0] + first[0] + 16) % 4 + 4 * (u // 2 + first[1])
        xk = jnp.where(u % 2 == 0, ids[1], 1 - ids[1])
        lst[n] = u
        return n + act[a, tile_of(zk, xk)]

    return lax.fori_loop(0, 2 * count, step, 0)


def load_units(ids, kv, bias, first, half, units):
    keys = [[kv[u // 2, u % 2, p] for u in units] for p in range(2)]
    b = []
    for u in units:
        zk = (ids[0] + first[0] + 16) % 4 + 4 * (u // 2 + first[1])
        xk = jnp.where(u % 2 == 0, ids[1], 1 - ids[1])
        b.append(bias[zk // 4, xk, jnp.where(half == 0, ids[1], 1 - ids[1]), zk % 4].astype(F32))
    keys = [k[0] if len(k) == 1 else jnp.concatenate(k, axis=0) for k in keys]
    return keys, b[0] if len(b) == 1 else jnp.concatenate(b, axis=0)


def over_units(ids, act, lst, first, count, half, body):
    a = tile_of(ids[0], jnp.where(half == 0, ids[1], 1 - ids[1]))
    n = list_units(ids, act, lst, a, first, count)

    @pl.loop(0, n // 2)
    def _(k):
        body([lst[2 * k], lst[2 * k + 1]])

    @pl.when(n % 2 == 1)
    def _():
        body([lst[n - 1]])


def stats_kernel(firsts, begin, end, ids, act, *refs):
    n = len(firsts)
    kvs, (bias, pack0, pack1), refs = refs[:n], refs[n : n + 3], refs[n + 3 :]
    before, refs = (None, refs) if begin else (refs[0], refs[1:])
    out, qd, lst, st = refs
    fill_queries(qd, (pack0, pack1))
    if begin:
        st[0] = jnp.full(st.shape[1:], NEG, F32)
        st[1:3] = jnp.zeros((2,) + st.shape[1:], F32)
    else:
        st[...] = before[...]

    @pl.loop(0, 2)
    def _(half):
        for kv, first in zip(kvs, firsts):

            def body(units, kv=kv, first=first):
                keys, b = load_units(ids, kv, bias, first, half, units)
                rows = b.shape[0] // 8
                for p in range(2):
                    sd = [nn(keys[p], qd[half, 2 * p + i]) for i in range(2)]
                    for i in range(2):
                        r = 2 * p + i
                        s = (sd[i][:, :128] + b).reshape(rows, 8, 128)
                        dp = sd[i][:, 128:].reshape(rows, 8, 128)
                        m_old = st[0, half, r]
                        m_new = jnp.maximum(m_old, jnp.max(s, axis=0))
                        e = jnp.exp(s - m_new[None])
                        c = jnp.exp(m_old - m_new)
                        st[1, half, r] = st[1, half, r] * c + jnp.sum(e, axis=0)
                        st[2, half, r] = st[2, half, r] * c + jnp.sum(e * dp, axis=0)
                        st[0, half, r] = m_new

            over_units(ids, act, lst, first, kv.shape[0], half, body)

    if not end:
        out[...] = st[...]
        return
    for half in range(2):
        for r in range(4):
            m = st[0, half, r]
            top = jnp.max(m, axis=0, keepdims=True)
            f = jnp.exp(m - top)
            total = jnp.sum(st[1, half, r] * f, axis=0, keepdims=True)
            out[half, r, 0:1] = top + jnp.log(total)
            out[half, r, 1:2] = jnp.sum(st[2, half, r] * f, axis=0, keepdims=True) / total


def back_kernel(firsts, ids, act, *refs):
    n = len(firsts)
    kvs, (bias, pack0, pack1, stats) = refs[:n], refs[n : n + 4]
    dkvs, (oq, qd, lst, acc) = refs[n + 4 : 2 * n + 4], refs[2 * n + 4 :]
    fill_queries(qd, (pack0, pack1))
    oq[...] = jnp.zeros_like(oq)
    for kv, dkv, first in zip(kvs, dkvs, firsts):
        count = kv.shape[0]
        acc[0:count] = jnp.zeros((count,) + acc.shape[1:], F32)

        @pl.loop(0, 2)
        def _(half):
            def body(units):
                keys, b = load_units(ids, kv, bias, first, half, units)
                for p in range(2):
                    keys_t = keys[p].T
                    qs = [qd[half, 2 * p + i] for i in range(2)]
                    sd = [nn(keys[p], q) for q in qs]
                    pds = []
                    for i in range(2):
                        r = 2 * p + i
                        prob = jnp.exp(sd[i][:, :128] + (b - stats[half, r, 0:1]))
                        dsc = prob * (sd[i][:, 128:] - stats[half, r, 1:2])
                        pds.append(jnp.concatenate([dsc.astype(BF16), prob.astype(BF16)], axis=1))
                    both = nt(jnp.concatenate(pds, axis=1), jnp.concatenate(qs, axis=1))
                    for k, u in enumerate(units):
                        acc[u // 2, u % 2, p] += both[128 * k : 128 * k + 128]
                    for i in range(2):
                        r = 2 * p + i
                        t = nn(keys_t[64 * i : 64 * i + 64], pds[i])
                        oq[half, r, 0:32] += t[0:32, 0:128]
                        oq[half, r, 32:64] += t[32:64, 128:256]

            over_units(ids, act, lst, first, count, half, body)

        dkv[...] = acc[0:count].astype(BF16)


def out_kernel(ids, oq_own, oq_other, gate, w_out, keep, send):
    xl, c = ids[1], ids[2]
    w_t = w_out[...].T
    for r in range(4):
        mine, theirs = oq_own[0, r, 32:64], oq_other[r, 32:64].astype(F32)
        att = jnp.concatenate(
            [jnp.where(xl == 0, mine, theirs), jnp.where(xl == 0, theirs, mine)], axis=0
        )
        part = nn(w_t, (gate[r] * att).astype(BF16))
        low, high = part[0:64], part[64:128]
        keep[r] = jnp.where(c == 0, low, high)
        send[r] = jnp.where(c == 0, high, low).astype(BF16)


def sum_kernel(d_own, r_up, r_down, r_up2, r_down2, out):
    for m in range(4):
        total = d_own[m].astype(F32) + r_up[m].astype(F32) + r_down[m].astype(F32)
        total += (r_up2[m] if m < 2 else r_down2[m - 2]).astype(F32)
        out[m] = total.astype(BF16)


def proj_kernel(ids, oq_own, oq_other, dkv_own, dkv_other, gate, go, w_proj, keep, send, dp):
    xl = ids[1]
    for p in range(2):
        mine_kv = sum(dkv_own[m, 0, p].astype(F32) for m in range(4)).T
        theirs_kv = dkv_other[p].astype(F32).T
        for i in range(2):
            r = 2 * p + i
            for oq, kvt, h in (
                (oq_own[0, r], mine_kv, xl),
                (oq_other[r].astype(F32), theirs_kv, 1 - xl),
            ):
                low = pl.multiple_of(h * DH, DH)
                g = gate[r, pl.ds(low, DH)]
                base = pl.multiple_of(h * 128, 128)
                dp[pl.ds(base, 32)] = oq[0:32]
                dp[pl.ds(base + 32, 64)] = kvt[64 * i : 64 * i + 64]
                dp[pl.ds(base + 96, 32)] = go[r, pl.ds(low, DH)] * oq[32:64] * g * (1.0 - g)
            part = nn(w_proj[...], dp[...].astype(BF16)).T
            keep[r] = part
            send[r] = part.astype(BF16)


def final_kernel(pair, gain, part, other, out):
    for r in range(4):
        xhat, inv = norm(pair[r].astype(F32))
        g = (part[r].astype(BF16).astype(F32) + other[r].astype(F32)) * gain[...]
        mean = jnp.mean(g, axis=-1, keepdims=True)
        along = jnp.mean(g * xhat, axis=-1, keepdims=True)
        out[r] = (inv * (g - mean - xhat * along)).astype(BF16)


def stats_call(firsts, begin, end, ids, active, kvs, rest):
    out = ((2, 4, 2, 128), F32) if end else ((3, 2, 4, 8, 128), F32)
    return call(
        functools.partial(stats_kernel, firsts, begin, end),
        [out],
        2,
        len(kvs) + len(rest),
        [
            pltpu.VMEM((2, 4, 128, 256), BF16),
            pltpu.SMEM((9,), jnp.int32),
            pltpu.VMEM((3, 2, 4, 8, 128), F32),
        ],
        flops=10 ** 9,
        nbytes=10 ** 7,
    )(ids, active, *kvs, *rest)[0]


def back_call(firsts, ids, active, kvs, rest):
    res = call(
        functools.partial(back_kernel, firsts),
        [(kv.shape, BF16) for kv in kvs] + [((2, 4, 64, 128), F32)],
        2,
        len(kvs) + len(rest),
        [
            pltpu.VMEM((2, 4, 128, 256), BF16),
            pltpu.SMEM((9,), jnp.int32),
            pltpu.VMEM((4, 2, 2, 128, 128), F32),
        ],
        flops=2 * 10 ** 9,
        nbytes=2 * 10 ** 7,
    )(ids, active, *kvs, *rest)
    return res[:-1], res[-1]


def to_z(x, step):
    return lax.ppermute(x, "z", [(j, (j + step) % 16) for j in range(16)])


def per_device(pair, gain, w_proj, w_out, tri_bias, active, d_out):
    ids = jnp.stack([lax.axis_index(name) for name in ("z", "xl", "c")]).astype(jnp.int32)
    gain = gain.reshape(1, 128)
    args = (pair, gain, w_proj, w_out, d_out, tri_bias)
    pack, pack_send, gate, go, bias = pl.pallas_call(
        prep_kernel,
        out_shape=shapes(
            *[((512, 128), BF16)] * 2, *[((4, 64, 128), F32)] * 2, ((4, 4, 128, 128), BF16)
        ),
        in_specs=[smem()] + [pl.BlockSpec(memory_space=pl.ANY)] * 6,
        out_specs=[vmem()] * 5,
        scratch_shapes=[pltpu.VMEM(a.shape, a.dtype) for a in args]
        + [pltpu.VMEM((2, 256, 128), F32), pltpu.SemaphoreType.DMA((6,))],
        compiler_params=pltpu.CompilerParams(vmem_limit_bytes=56 * 1024 * 1024),
    )(ids, *args)
    pack_other = lax.ppermute(pack_send, "xl", SWAP)
    bias = lax.all_to_all(bias, ("xh", "xl"), 0, 0, tiled=True).reshape(2, 2, 4, 128, 128)
    bias, pack_other = lax.optimization_barrier((bias, pack_other))
    bias = lax.all_gather(bias, "y")
    kv = jnp.stack([pack[:256].reshape(2, 128, 128), pack_other[:256].reshape(2, 128, 128)])
    groups = [[k + 4 * m for m in range(4)] for k in range(4)]
    own = lax.all_gather(kv, "z", axis_index_groups=groups)
    up, down = to_z(own, -1), to_z(own, 1)
    up2, down2 = to_z(own[0:2], -2), to_z(own[2:4], 2)
    rest = (bias, pack, pack_other)
    state = stats_call(((0, 0),), True, False, ids, active, (own,), rest)
    state = stats_call(((1, 0), (-1, 0)), False, False, ids, active, (up, down), rest + (state,))
    stats = stats_call(((2, 0), (-2, 2)), False, True, ids, active, (up2, down2), rest + (state,))
    (d_up,), oq1 = back_call(((1, 0),), ids, active, (up,), rest + (stats,))
    r_up = to_z(d_up, 1)
    (d_down,), oq3 = back_call(((-1, 0),), ids, active, (down,), rest + (stats,))
    r_down = to_z(d_down, -1)
    (d_up2, d_down2), oq2 = back_call(((2, 0), (-2, 2)), ids, active, (up2, down2), rest + (stats,))
    r_up2, r_down2 = to_z(d_up2, 2), to_z(d_down2, -2)
    (d_own,), oq0 = back_call(((0, 0),), ids, active, (own,), rest + (stats,))
    oq = oq0 + oq1 + oq2 + oq3
    oq = jnp.concatenate([oq[:, :, :32] * SCALE, oq[:, :, 32:]], axis=2)
    oq_other = lax.ppermute(oq[1].astype(BF16), "xl", SWAP)
    out_keep, out_send = call(
        out_kernel, [((4, 64, 128), F32), ((4, 64, 128), BF16)], 1, 4
    )(ids, oq, oq_other, gate, w_out)
    out_other = lax.ppermute(out_send, "c", SWAP)
    out = (out_keep + out_other.astype(F32)).astype(BF16)
    (sums,) = call(sum_kernel, [((4, 2, 2, 128, 128), BF16)], 0, 5)(
        d_own, r_up, r_down, r_up2, r_down2
    )
    dkv = lax.all_to_all(sums, "z", 0, 0, axis_index_groups=groups, tiled=True)
    dkv, _ = lax.optimization_barrier((dkv, out_other))
    theirs = jnp.sum(dkv[:, 1].astype(F32), axis=0).astype(BF16)
    dkv_other = lax.ppermute(theirs, "xl", SWAP)
    part, part_send = call(
        proj_kernel,
        [((4, 128, 128), F32), ((4, 128, 128), BF16)],
        1,
        7,
        [pltpu.VMEM((256, 128), F32)],
    )(ids, oq, oq_other, dkv, dkv_other, gate, go, w_proj)
    (pair_gradient,) = call(final_kernel, [((4, 128, 128), BF16)], 0, 4)(
        pair, gain, part, lax.ppermute(part_send, "c", SWAP)
    )
    return jnp.swapaxes(out, 1, 2), pair_gradient


def solution(mesh):
    fine = Mesh(np.asarray(mesh.devices).reshape(2, 4, 2, 16, 2), ("xh", "y", "xl", "z", "c"))
    row, col = ("xh", "y"), ("xl", "z")
    return jax.shard_map(
        per_device,
        mesh=fine,
        in_specs=(
            P(row, col, None),
            P(),
            P(None, "c"),
            P("c", None),
            P("c", col, row),
            P(),
            P(row, col, None),
        ),
        out_specs=(P(row, col, "c"), P(row, col, None)),
        check_vma=False,
    )
```

```python
import functools

import jax
import jax.numpy as jnp
import numpy as np
from jax import lax
from jax.experimental import pallas as pl
from jax.experimental.pallas import tpu as pltpu
from jax.sharding import Mesh
from jax.sharding import PartitionSpec as P

DH = 32
SCALE = DH ** (-0.5)
EPS = 1e-05
NEG = -1e30
F32 = jnp.float32
BF16 = jnp.bfloat16
SWAP = [(0, 1), (1, 0)]
OWN, UP, DOWN, UP2, DOWN2 = range(5)
ARRAYS = ((0, 0, 4), (1, 0, 4), (-1, 0, 4), (2, 0, 2), (-2, 2, 2))


def vmem():
    return pl.BlockSpec(memory_space=pltpu.VMEM)


def smem():
    return pl.BlockSpec(memory_space=pltpu.SMEM)


def shapes(*items):
    return [jax.ShapeDtypeStruct(s, d) for s, d in items]


def call(kernel, outs, n_smem, n_vmem, scratch=(), flops=0, nbytes=0):
    return pl.pallas_call(
        kernel,
        out_shape=shapes(*outs),
        in_specs=[smem()] * n_smem + [vmem()] * n_vmem,
        out_specs=[vmem()] * len(outs),
        scratch_shapes=list(scratch),
        compiler_params=pltpu.CompilerParams(vmem_limit_bytes=24 * 1024 * 1024),
        cost_estimate=pl.CostEstimate(flops=flops, bytes_accessed=nbytes, transcendentals=0),
    )


def nt(a, b):
    return lax.dot_general(a, b, (((1,), (1,)), ((), ())), preferred_element_type=F32)


def nn(a, b):
    return jnp.dot(a, b, preferred_element_type=F32)


def norm(x):
    mean = jnp.mean(x, axis=-1, keepdims=True)
    centred = x - mean
    inv = lax.rsqrt(jnp.mean(centred * centred, axis=-1, keepdims=True) + EPS)
    return centred * inv, inv


def prep_kernel(ids, *refs):
    here, (keep, send, gate_out, go_out, bias_out) = refs[:6], refs[6:11]
    pair, gain, w_proj, w_out, d_out, bias = local = refs[11:17]
    proj_s, sems = refs[17:]
    copies = [pltpu.make_async_copy(s, d, sems.at[k]) for k, (s, d) in enumerate(zip(here, local))]
    for copy in copies:
        copy.start()
    for copy in copies[:5]:
        copy.wait()
    xl = ids[1]
    w_t = w_proj[...].T
    for p in range(2):
        for i in range(2):
            r = 2 * p + i
            xhat, _ = norm(pair[r].astype(F32))
            normed = (xhat * gain[...]).astype(BF16)
            proj = nt(w_t, normed)
            go = nt(w_out[...], d_out[r])
            go_out[r] = go
            for h in range(2):
                gate = jax.nn.sigmoid(proj[h * 128 + 96 : h * 128 + 128])
                gate_out[r, h * DH : (h + 1) * DH] = gate
                proj_s[h, i * 64 : (i + 1) * 64] = proj[h * 128 + 32 : h * 128 + 96]
                proj_s[h, 128 + i * 64 : 160 + i * 64] = proj[h * 128 : h * 128 + 32] * SCALE
                proj_s[h, 160 + i * 64 : 192 + i * 64] = go[h * DH : (h + 1) * DH] * gate
        for ref, h in ((keep, xl), (send, 1 - xl)):
            ref[p * 128 : (p + 1) * 128] = proj_s[h, 0:128].T.astype(BF16)
            ref[256 + p * 128 : 384 + p * 128] = proj_s[h, 128:256].astype(BF16)
    copies[5].wait()
    for j in range(4):
        for h in range(2):
            block = bias[h, :, 128 * j : 128 * j + 128].T
            bias_out[h, j] = block
            bias_out[2 + h, j] = block


def fill_queries(qd, packs):
    qd[...] = jnp.zeros_like(qd)
    for half, pack in enumerate(packs):
        for r in range(4):
            low = 64 * (r % 2)
            qd[half, r, low : low + 32, 0:128] = pack[256 + 64 * r : 288 + 64 * r]
            qd[half, r, low + 32 : low + 64, 128:256] = pack[288 + 64 * r : 320 + 64 * r]


def tile_of(zk, xk):
    return zk // 2 + 8 * xk


def setup_kernel(ids, act, pack0, pack1, lists, qd):
    fill_queries(qd, (pack0, pack1))
    for k, (step, low, count) in enumerate(ARRAYS):
        for half in range(2):
            a = tile_of(ids[0], ids[1] if half == 0 else 1 - ids[1])
            base = 9 * (2 * k + half)
            n = 0
            for u in range(2 * count):
                zk = (ids[0] + step + 16) % 4 + 4 * (u // 2 + low)
                xk = ids[1] if u % 2 == 0 else 1 - ids[1]
                lists[base + n] = u
                n = n + act[a, tile_of(zk, xk)]
            lists[base + 8] = n


def load_units(ids, kv, bias, which, half, units):
    step, low, _ = ARRAYS[which]
    keys = [[kv[u // 2, u % 2, p] for u in units] for p in range(2)]
    b = []
    for u in units:
        xk = jnp.where(u % 2 == 0, ids[1], 1 - ids[1])
        xq = jnp.where(half == 0, ids[1], 1 - ids[1])
        b.append(bias[u // 2 + low, xk, xq, (ids[0] + step + 16) % 4].astype(F32))
    keys = [k[0] if len(k) == 1 else jnp.concatenate(k, axis=0) for k in keys]
    return keys, b[0] if len(b) == 1 else jnp.concatenate(b, axis=0)


def over_units(lists, which, half, body):
    base = 9 * (2 * which + half)
    n = lists[base + 8]

    @pl.loop(0, n // 2)
    def _(k):
        body([lists[base + 2 * k], lists[base + 2 * k + 1]])

    @pl.when(n % 2 == 1)
    def _():
        body([lists[base + n - 1]])


def stats_kernel(names, begin, end, ids, lists, *refs):
    n = len(names)
    kvs, (bias, qd), refs = refs[:n], refs[n : n + 2], refs[n + 2 :]
    before, refs = (None, refs) if begin else (refs[0], refs[1:])
    out, st = refs
    if begin:
        st[0] = jnp.full(st.shape[1:], NEG, F32)
        st[1:3] = jnp.zeros((2,) + st.shape[1:], F32)
    else:
        st[...] = before[...]

    @pl.loop(0, 2)
    def _(half):
        for kv, which in zip(kvs, names):

            def body(units, kv=kv, which=which):
                keys, b = load_units(ids, kv, bias, which, half, units)
                rows = b.shape[0] // 8
                for p in range(2):
                    sd = [nn(keys[p], qd[half, 2 * p + i]) for i in range(2)]
                    for i in range(2):
                        r = 2 * p + i
                        s = (sd[i][:, :128] + b).reshape(rows, 8, 128)
                        dp = sd[i][:, 128:].reshape(rows, 8, 128)
                        m_old = st[0, half, r]
                        m_new = jnp.maximum(m_old, jnp.max(s, axis=0))
                        e = jnp.exp(s - m_new[None])
                        c = jnp.exp(m_old - m_new)
                        st[1, half, r] = st[1, half, r] * c + jnp.sum(e, axis=0)
                        st[2, half, r] = st[2, half, r] * c + jnp.sum(e * dp, axis=0)
                        st[0, half, r] = m_new

            over_units(lists, which, half, body)

    if not end:
        out[...] = st[...]
        return
    for half in range(2):
        for r in range(4):
            m = st[0, half, r]
            top = jnp.max(m, axis=0, keepdims=True)
            f = jnp.exp(m - top)
            total = jnp.sum(st[1, half, r] * f, axis=0, keepdims=True)
            out[half, r, 0:1] = top + jnp.log(total)
            out[half, r, 1:2] = jnp.sum(st[2, half, r] * f, axis=0, keepdims=True) / total


def back_kernel(names, ids, lists, *refs):
    n = len(names)
    kvs, (bias, qd, stats) = refs[:n], refs[n : n + 3]
    dkvs, (oq, acc) = refs[n + 3 : 2 * n + 3], refs[2 * n + 3 :]
    oq[...] = jnp.zeros_like(oq)
    for kv, dkv, which in zip(kvs, dkvs, names):
        count = kv.shape[0]
        acc[0:count] = jnp.zeros((count,) + acc.shape[1:], F32)

        @pl.loop(0, 2)
        def _(half):
            def body(units):
                keys, b = load_units(ids, kv, bias, which, half, units)
                for p in range(2):
                    keys_t = keys[p].T
                    qs = [qd[half, 2 * p + i] for i in range(2)]
                    sd = [nn(keys[p], q) for q in qs]
                    pds = []
                    for i in range(2):
                        r = 2 * p + i
                        prob = jnp.exp(sd[i][:, :128] + (b - stats[half, r, 0:1]))
                        dsc = prob * (sd[i][:, 128:] - stats[half, r, 1:2])
                        pds.append(jnp.concatenate([dsc.astype(BF16), prob.astype(BF16)], axis=1))
                    both = nt(jnp.concatenate(pds, axis=1), jnp.concatenate(qs, axis=1))
                    for k, u in enumerate(units):
                        acc[u // 2, u % 2, p] += both[128 * k : 128 * k + 128]
                    for i in range(2):
                        r = 2 * p + i
                        t = nn(keys_t[64 * i : 64 * i + 64], pds[i])
                        oq[half, r, 0:32] += t[0:32, 0:128]
                        oq[half, r, 32:64] += t[32:64, 128:256]

            over_units(lists, which, half, body)

        dkv[...] = acc[0:count].astype(BF16)


def out_kernel(ids, oq_own, oq_other, gate, w_out, keep, send):
    xl, c = ids[1], ids[2]
    w_t = w_out[...].T
    for r in range(4):
        mine, theirs = oq_own[0, r, 32:64], oq_other[r, 32:64].astype(F32)
        att = jnp.concatenate(
            [jnp.where(xl == 0, mine, theirs), jnp.where(xl == 0, theirs, mine)], axis=0
        )
        part = nn(w_t, (gate[r] * att).astype(BF16))
        low, high = part[0:64], part[64:128]
        keep[r] = jnp.where(c == 0, low, high)
        send[r] = jnp.where(c == 0, high, low).astype(BF16)


def sum_kernel(d_own, r_up, r_down, r_up2, r_down2, out):
    for m in range(4):
        total = d_own[m].astype(F32) + r_up[m].astype(F32) + r_down[m].astype(F32)
        total += (r_up2[m] if m < 2 else r_down2[m - 2]).astype(F32)
        out[m] = total.astype(BF16)


def proj_kernel(ids, oq_own, oq_other, dkv_own, dkv_other, gate, go, w_proj, keep, send, dp):
    xl = ids[1]
    for p in range(2):
        mine_kv = sum(dkv_own[m, 0, p].astype(F32) for m in range(4)).T
        theirs_kv = dkv_other[p].astype(F32).T
        for i in range(2):
            r = 2 * p + i
            for oq, kvt, h in (
                (oq_own[0, r], mine_kv, xl),
                (oq_other[r].astype(F32), theirs_kv, 1 - xl),
            ):
                low = pl.multiple_of(h * DH, DH)
                g = gate[r, pl.ds(low, DH)]
                base = pl.multiple_of(h * 128, 128)
                dp[pl.ds(base, 32)] = oq[0:32]
                dp[pl.ds(base + 32, 64)] = kvt[64 * i : 64 * i + 64]
                dp[pl.ds(base + 96, 32)] = go[r, pl.ds(low, DH)] * oq[32:64] * g * (1.0 - g)
            part = nn(w_proj[...], dp[...].astype(BF16)).T
            keep[r] = part
            send[r] = part.astype(BF16)


def final_kernel(pair, gain, part, other, out):
    for r in range(4):
        xhat, inv = norm(pair[r].astype(F32))
        g = (part[r].astype(BF16).astype(F32) + other[r].astype(F32)) * gain[...]
        mean = jnp.mean(g, axis=-1, keepdims=True)
        along = jnp.mean(g * xhat, axis=-1, keepdims=True)
        out[r] = (inv * (g - mean - xhat * along)).astype(BF16)


def stats_call(names, begin, end, ids, lists, kvs, rest):
    out = ((2, 4, 2, 128), F32) if end else ((3, 2, 4, 8, 128), F32)
    return call(
        functools.partial(stats_kernel, names, begin, end),
        [out],
        2,
        len(kvs) + len(rest),
        [pltpu.VMEM((3, 2, 4, 8, 128), F32)],
        flops=10 ** 9,
        nbytes=10 ** 7,
    )(ids, lists, *kvs, *rest)[0]


def back_call(names, ids, lists, kvs, rest):
    res = call(
        functools.partial(back_kernel, names),
        [(kv.shape, BF16) for kv in kvs] + [((2, 4, 64, 128), F32)],
        2,
        len(kvs) + len(rest),
        [pltpu.VMEM((4, 2, 2, 128, 128), F32)],
        flops=2 * 10 ** 9,
        nbytes=2 * 10 ** 7,
    )(ids, lists, *kvs, *rest)
    return res[:-1], res[-1]


def to_z(x, step):
    return lax.ppermute(x, "z", [(j, (j + step) % 16) for j in range(16)])


def per_device(pair, gain, w_proj, w_out, tri_bias, active, d_out):
    ids = jnp.stack([lax.axis_index(name) for name in ("z", "xl", "c")]).astype(jnp.int32)
    gain = gain.reshape(1, 128)
    args = (pair, gain, w_proj, w_out, d_out, tri_bias)
    pack, pack_send, gate, go, bias = pl.pallas_call(
        prep_kernel,
        out_shape=shapes(
            *[((512, 128), BF16)] * 2, *[((4, 64, 128), F32)] * 2, ((4, 4, 128, 128), BF16)
        ),
        in_specs=[smem()] + [pl.BlockSpec(memory_space=pl.ANY)] * 6,
        out_specs=[vmem()] * 5,
        scratch_shapes=[pltpu.VMEM(a.shape, a.dtype) for a in args]
        + [pltpu.VMEM((2, 256, 128), F32), pltpu.SemaphoreType.DMA((6,))],
        compiler_params=pltpu.CompilerParams(vmem_limit_bytes=56 * 1024 * 1024),
    )(ids, *args)
    pack_other = lax.ppermute(pack_send, "xl", SWAP)
    bias = lax.all_to_all(bias, ("xh", "xl"), 0, 0, tiled=True).reshape(2, 2, 4, 128, 128)
    bias, pack_other = lax.optimization_barrier((bias, pack_other))
    bias = lax.all_gather(bias, "y")
    kv = jnp.stack([pack[:256].reshape(2, 128, 128), pack_other[:256].reshape(2, 128, 128)])
    groups = [[k + 4 * m for m in range(4)] for k in range(4)]
    own = lax.all_gather(kv, "z", axis_index_groups=groups)
    up, down = to_z(own, -1), to_z(own, 1)
    up2, down2 = to_z(own[0:2], -2), to_z(own[2:4], 2)
    lists, qd = pl.pallas_call(
        setup_kernel,
        out_shape=shapes(((90,), jnp.int32), ((2, 4, 128, 256), BF16)),
        in_specs=[smem()] * 2 + [vmem()] * 2,
        out_specs=[smem(), vmem()],
        compiler_params=pltpu.CompilerParams(vmem_limit_bytes=24 * 1024 * 1024),
    )(ids, active, pack, pack_other)
    rest = (bias, qd)
    state = stats_call((OWN,), True, False, ids, lists, (own,), rest)
    stats = stats_call(
        (UP, DOWN, UP2, DOWN2), False, True, ids, lists, (up, down, up2, down2), rest + (state,)
    )
    rest = rest + (stats,)
    (d_up2, d_down2), oq2 = back_call((UP2, DOWN2), ids, lists, (up2, down2), rest)
    r_up2, r_down2 = to_z(d_up2, 2), to_z(d_down2, -2)
    (d_up,), oq1 = back_call((UP,), ids, lists, (up,), rest)
    r_up = to_z(d_up, 1)
    (d_down,), oq3 = back_call((DOWN,), ids, lists, (down,), rest)
    r_down = to_z(d_down, -1)
    (d_own,), oq0 = back_call((OWN,), ids, lists, (own,), rest)
    oq = oq0 + oq1 + oq2 + oq3
    oq = jnp.concatenate([oq[:, :, :32] * SCALE, oq[:, :, 32:]], axis=2)
    oq_other = lax.ppermute(oq[1].astype(BF16), "xl", SWAP)
    out_keep, out_send = call(
        out_kernel, [((4, 64, 128), F32), ((4, 64, 128), BF16)], 1, 4
    )(ids, oq, oq_other, gate, w_out)
    out_other = lax.ppermute(out_send, "c", SWAP)
    out = (out_keep + out_other.astype(F32)).astype(BF16)
    (sums,) = call(sum_kernel, [((4, 2, 2, 128, 128), BF16)], 0, 5)(
        d_own, r_up, r_down, r_up2, r_down2
    )
    dkv = lax.all_to_all(sums, "z", 0, 0, axis_index_groups=groups, tiled=True)
    dkv, _ = lax.optimization_barrier((dkv, out_other))
    theirs = jnp.sum(dkv[:, 1].astype(F32), axis=0).astype(BF16)
    dkv_other = lax.ppermute(theirs, "xl", SWAP)
    part, part_send = call(
        proj_kernel,
        [((4, 128, 128), F32), ((4, 128, 128), BF16)],
        1,
        7,
        [pltpu.VMEM((256, 128), F32)],
    )(ids, oq, oq_other, dkv, dkv_other, gate, go, w_proj)
    (pair_gradient,) = call(final_kernel, [((4, 128, 128), BF16)], 0, 4)(
        pair, gain, part, lax.ppermute(part_send, "c", SWAP)
    )
    return jnp.swapaxes(out, 1, 2), pair_gradient


def solution(mesh):
    fine = Mesh(np.asarray(mesh.devices).reshape(2, 4, 2, 16, 2), ("xh", "y", "xl", "z", "c"))
    row, col = ("xh", "y"), ("xl", "z")
    return jax.shard_map(
        per_device,
        mesh=fine,
        in_specs=(
            P(row, col, None),
            P(),
            P(None, "c"),
            P("c", None),
            P("c", col, row),
            P(),
            P(row, col, None),
        ),
        out_specs=(P(row, col, "c"), P(row, col, None)),
        check_vma=False,
    )
```

```python
import functools

import jax
import jax.numpy as jnp
import numpy as np
from jax import lax
from jax.experimental import pallas as pl
from jax.experimental.pallas import tpu as pltpu
from jax.sharding import Mesh
from jax.sharding import PartitionSpec as P

DH = 32
SCALE = DH ** (-0.5)
EPS = 1e-05
NEG = -1e30
F32 = jnp.float32
BF16 = jnp.bfloat16
SWAP = [(0, 1), (1, 0)]
OWN, UP, DOWN, UP2, DOWN2 = range(5)
ARRAYS = ((0, 0, 4), (1, 0, 4), (-1, 0, 4), (2, 0, 2), (-2, 2, 2))


def place():
    return [lax.axis_index(name) for name in ("z", "xl", "c")]


def vmem():
    return pl.BlockSpec(memory_space=pltpu.VMEM)


def smem():
    return pl.BlockSpec(memory_space=pltpu.SMEM)


def shapes(*items):
    return [jax.ShapeDtypeStruct(s, d) for s, d in items]


def call(kernel, outs, n_smem, n_vmem, scratch=(), flops=0, nbytes=0):
    return pl.pallas_call(
        kernel,
        out_shape=shapes(*outs),
        in_specs=[smem()] * n_smem + [vmem()] * n_vmem,
        out_specs=[vmem()] * len(outs),
        scratch_shapes=list(scratch),
        compiler_params=pltpu.CompilerParams(vmem_limit_bytes=24 * 1024 * 1024),
        cost_estimate=pl.CostEstimate(flops=flops, bytes_accessed=nbytes, transcendentals=0),
    )


def nt(a, b):
    return lax.dot_general(a, b, (((1,), (1,)), ((), ())), preferred_element_type=F32)


def nn(a, b):
    return jnp.dot(a, b, preferred_element_type=F32)


def norm(x):
    mean = jnp.mean(x, axis=-1, keepdims=True)
    centred = x - mean
    inv = lax.rsqrt(jnp.mean(centred * centred, axis=-1, keepdims=True) + EPS)
    return centred * inv, inv


def prep_kernel(*refs):
    ids = place()
    here, (keep, send, gate_out, go_out, bias_out) = refs[:6], refs[6:11]
    pair, gain, w_proj, w_out, d_out, bias = local = refs[11:17]
    proj_s, sems = refs[17:]
    copies = [pltpu.make_async_copy(s, d, sems.at[k]) for k, (s, d) in enumerate(zip(here, local))]
    for copy in copies:
        copy.start()
    for copy in copies[:5]:
        copy.wait()
    xl = ids[1]
    w_t = w_proj[...].T
    for p in range(2):
        for i in range(2):
            r = 2 * p + i
            xhat, _ = norm(pair[r].astype(F32))
            normed = (xhat * gain[...]).astype(BF16)
            proj = nt(w_t, normed)
            go = nt(w_out[...], d_out[r])
            go_out[r] = go
            for h in range(2):
                gate = jax.nn.sigmoid(proj[h * 128 + 96 : h * 128 + 128])
                gate_out[r, h * DH : (h + 1) * DH] = gate
                proj_s[h, i * 64 : (i + 1) * 64] = proj[h * 128 + 32 : h * 128 + 96]
                proj_s[h, 128 + i * 64 : 160 + i * 64] = proj[h * 128 : h * 128 + 32] * SCALE
                proj_s[h, 160 + i * 64 : 192 + i * 64] = go[h * DH : (h + 1) * DH] * gate
        for ref, h in ((keep, xl), (send, 1 - xl)):
            ref[p * 128 : (p + 1) * 128] = proj_s[h, 0:128].T.astype(BF16)
            ref[256 + p * 128 : 384 + p * 128] = proj_s[h, 128:256].astype(BF16)
    copies[5].wait()
    for j in range(4):
        for h in range(2):
            block = bias[h, :, 128 * j : 128 * j + 128].T
            bias_out[h, j] = block
            bias_out[2 + h, j] = block


def fill_queries(qd, packs):
    qd[...] = jnp.zeros_like(qd)
    for half, pack in enumerate(packs):
        for r in range(4):
            low = 64 * (r % 2)
            qd[half, r, low : low + 32, 0:128] = pack[256 + 64 * r : 288 + 64 * r]
            qd[half, r, low + 32 : low + 64, 128:256] = pack[288 + 64 * r : 320 + 64 * r]


def tile_of(zk, xk):
    return zk // 2 + 8 * xk


def setup_kernel(act, pack0, pack1, lists, qd):
    ids = place()
    fill_queries(qd, (pack0, pack1))
    for k, (step, low, count) in enumerate(ARRAYS):
        for half in range(2):
            a = tile_of(ids[0], ids[1] if half == 0 else 1 - ids[1])
            base = 9 * (2 * k + half)
            n = 0
            for u in range(2 * count):
                zk = (ids[0] + step + 16) % 4 + 4 * (u // 2 + low)
                xk = ids[1] if u % 2 == 0 else 1 - ids[1]
                lists[base + n] = u
                n = n + act[a, tile_of(zk, xk)]
            lists[base + 8] = n


def load_units(ids, kv, bias, which, half, units):
    step, low, _ = ARRAYS[which]
    keys = [[kv[u // 2, u % 2, p] for u in units] for p in range(2)]
    b = []
    for u in units:
        xk = jnp.where(u % 2 == 0, ids[1], 1 - ids[1])
        xq = jnp.where(half == 0, ids[1], 1 - ids[1])
        b.append(bias[u // 2 + low, xk, xq, (ids[0] + step + 16) % 4].astype(F32))
    keys = [k[0] if len(k) == 1 else jnp.concatenate(k, axis=0) for k in keys]
    return keys, b[0] if len(b) == 1 else jnp.concatenate(b, axis=0)


def over_units(lists, which, half, body):
    base = 9 * (2 * which + half)
    n = lists[base + 8]

    @pl.loop(0, n // 2)
    def _(k):
        body([lists[base + 2 * k], lists[base + 2 * k + 1]])

    @pl.when(n % 2 == 1)
    def _():
        body([lists[base + n - 1]])


def stats_kernel(names, begin, end, lists, *refs):
    n, ids = len(names), place()
    kvs, (bias, qd), refs = refs[:n], refs[n : n + 2], refs[n + 2 :]
    before, refs = (None, refs) if begin else (refs[0], refs[1:])
    out, st = refs
    if begin:
        st[0] = jnp.full(st.shape[1:], NEG, F32)
        st[1:3] = jnp.zeros((2,) + st.shape[1:], F32)
    else:
        st[...] = before[...]

    @pl.loop(0, 2)
    def _(half):
        for kv, which in zip(kvs, names):

            def body(units, kv=kv, which=which):
                keys, b = load_units(ids, kv, bias, which, half, units)
                rows = b.shape[0] // 8
                for p in range(2):
                    sd = [nn(keys[p], qd[half, 2 * p + i]) for i in range(2)]
                    for i in range(2):
                        r = 2 * p + i
                        s = (sd[i][:, :128] + b).reshape(rows, 8, 128)
                        dp = sd[i][:, 128:].reshape(rows, 8, 128)
                        m_old = st[0, half, r]
                        m_new = jnp.maximum(m_old, jnp.max(s, axis=0))
                        e = jnp.exp(s - m_new[None])
                        c = jnp.exp(m_old - m_new)
                        st[1, half, r] = st[1, half, r] * c + jnp.sum(e, axis=0)
                        st[2, half, r] = st[2, half, r] * c + jnp.sum(e * dp, axis=0)
                        st[0, half, r] = m_new

            over_units(lists, which, half, body)

    if not end:
        out[...] = st[...]
        return
    for half in range(2):
        for r in range(4):
            m = st[0, half, r]
            top = jnp.max(m, axis=0, keepdims=True)
            f = jnp.exp(m - top)
            total = jnp.sum(st[1, half, r] * f, axis=0, keepdims=True)
            out[half, r, 0:1] = top + jnp.log(total)
            out[half, r, 1:2] = jnp.sum(st[2, half, r] * f, axis=0, keepdims=True) / total


def back_kernel(names, lists, *refs):
    n, ids = len(names), place()
    kvs, (bias, qd, stats) = refs[:n], refs[n : n + 3]
    dkvs, (oq, acc) = refs[n + 3 : 2 * n + 3], refs[2 * n + 3 :]
    oq[...] = jnp.zeros_like(oq)
    for kv, dkv, which in zip(kvs, dkvs, names):
        count = kv.shape[0]
        acc[0:count] = jnp.zeros((count,) + acc.shape[1:], F32)

        @pl.loop(0, 2)
        def _(half):
            def body(units):
                keys, b = load_units(ids, kv, bias, which, half, units)
                for p in range(2):
                    keys_t = keys[p].T
                    qs = [qd[half, 2 * p + i] for i in range(2)]
                    sd = [nn(keys[p], q) for q in qs]
                    pds = []
                    for i in range(2):
                        r = 2 * p + i
                        prob = jnp.exp(sd[i][:, :128] + (b - stats[half, r, 0:1]))
                        dsc = prob * (sd[i][:, 128:] - stats[half, r, 1:2])
                        pds.append(jnp.concatenate([dsc.astype(BF16), prob.astype(BF16)], axis=1))
                    both = nt(jnp.concatenate(pds, axis=1), jnp.concatenate(qs, axis=1))
                    for k, u in enumerate(units):
                        acc[u // 2, u % 2, p] += both[128 * k : 128 * k + 128]
                    for i in range(2):
                        r = 2 * p + i
                        t = nn(keys_t[64 * i : 64 * i + 64], pds[i])
                        oq[half, r, 0:32] += t[0:32, 0:128]
                        oq[half, r, 32:64] += t[32:64, 128:256]

            over_units(lists, which, half, body)

        dkv[...] = acc[0:count].astype(BF16)


def out_kernel(oq_own, oq_other, gate, w_out, keep, send):
    _, xl, c = place()
    w_t = w_out[...].T
    for r in range(4):
        mine, theirs = oq_own[0, r, 32:64], oq_other[r, 32:64].astype(F32)
        att = jnp.concatenate(
            [jnp.where(xl == 0, mine, theirs), jnp.where(xl == 0, theirs, mine)], axis=0
        )
        part = nn(w_t, (gate[r] * att).astype(BF16))
        low, high = part[0:64], part[64:128]
        keep[r] = jnp.where(c == 0, low, high)
        send[r] = jnp.where(c == 0, high, low).astype(BF16)


def sum_kernel(d_own, r_up, r_down, r_up2, r_down2, own, other):
    for m in range(4):
        total = d_own[m].astype(F32) + r_up[m].astype(F32) + r_down[m].astype(F32)
        total += (r_up2[m] if m < 2 else r_down2[m - 2]).astype(F32)
        own[m], other[m] = total[0].astype(BF16), total[1].astype(BF16)


def proj_kernel(oq_own, oq_other, dkv_own, dkv_other, gate, go, w_proj, keep, send, dp):
    _, xl, _ = place()
    for p in range(2):
        mine_kv = sum(dkv_own[m, p].astype(F32) for m in range(4)).T
        theirs_kv = dkv_other[p].astype(F32).T
        for i in range(2):
            r = 2 * p + i
            for oq, kvt, h in (
                (oq_own[0, r], mine_kv, xl),
                (oq_other[r].astype(F32), theirs_kv, 1 - xl),
            ):
                low = pl.multiple_of(h * DH, DH)
                g = gate[r, pl.ds(low, DH)]
                base = pl.multiple_of(h * 128, 128)
                dp[pl.ds(base, 32)] = oq[0:32]
                dp[pl.ds(base + 32, 64)] = kvt[64 * i : 64 * i + 64]
                dp[pl.ds(base + 96, 32)] = go[r, pl.ds(low, DH)] * oq[32:64] * g * (1.0 - g)
            part = nn(w_proj[...], dp[...].astype(BF16)).T
            keep[r] = part
            send[r] = part.astype(BF16)


def final_kernel(pair, gain, part, other, out):
    for r in range(4):
        xhat, inv = norm(pair[r].astype(F32))
        g = (part[r].astype(BF16).astype(F32) + other[r].astype(F32)) * gain[...]
        mean = jnp.mean(g, axis=-1, keepdims=True)
        along = jnp.mean(g * xhat, axis=-1, keepdims=True)
        out[r] = (inv * (g - mean - xhat * along)).astype(BF16)


def stats_call(names, begin, end, lists, kvs, rest):
    out = ((2, 4, 2, 128), F32) if end else ((3, 2, 4, 8, 128), F32)
    return call(
        functools.partial(stats_kernel, names, begin, end),
        [out],
        1,
        len(kvs) + len(rest),
        [pltpu.VMEM((3, 2, 4, 8, 128), F32)],
        flops=10 ** 9,
        nbytes=10 ** 7,
    )(lists, *kvs, *rest)[0]


def back_call(names, lists, kvs, rest):
    res = call(
        functools.partial(back_kernel, names),
        [(kv.shape, BF16) for kv in kvs] + [((2, 4, 64, 128), F32)],
        1,
        len(kvs) + len(rest),
        [pltpu.VMEM((4, 2, 2, 128, 128), F32)],
        flops=2 * 10 ** 9,
        nbytes=2 * 10 ** 7,
    )(lists, *kvs, *rest)
    return res[:-1], res[-1]


def to_z(x, step):
    return lax.ppermute(x, "z", [(j, (j + step) % 16) for j in range(16)])


def per_device(pair, gain, w_proj, w_out, tri_bias, active, d_out):
    gain = gain.reshape(1, 128)
    args = (pair, gain, w_proj, w_out, d_out, tri_bias)
    pack, pack_send, gate, go, bias = pl.pallas_call(
        prep_kernel,
        out_shape=shapes(
            *[((512, 128), BF16)] * 2, *[((4, 64, 128), F32)] * 2, ((4, 4, 128, 128), BF16)
        ),
        in_specs=[pl.BlockSpec(memory_space=pl.ANY)] * 6,
        out_specs=[vmem()] * 5,
        scratch_shapes=[pltpu.VMEM(a.shape, a.dtype) for a in args]
        + [pltpu.VMEM((2, 256, 128), F32), pltpu.SemaphoreType.DMA((6,))],
        compiler_params=pltpu.CompilerParams(vmem_limit_bytes=56 * 1024 * 1024),
    )(*args)
    pack_other = lax.ppermute(pack_send, "xl", SWAP)
    bias = lax.all_to_all(bias, ("xh", "xl"), 0, 0, tiled=True).reshape(2, 2, 4, 128, 128)
    bias, pack_other = lax.optimization_barrier((bias, pack_other))
    bias = lax.all_gather(bias, "y")
    kv = jnp.stack([pack[:256].reshape(2, 128, 128), pack_other[:256].reshape(2, 128, 128)])
    groups = [[k + 4 * m for m in range(4)] for k in range(4)]
    own = lax.all_gather(kv, "z", axis_index_groups=groups)
    up, down = to_z(own, -1), to_z(own, 1)
    up2, down2 = to_z(own[0:2], -2), to_z(own[2:4], 2)
    lists, qd = pl.pallas_call(
        setup_kernel,
        out_shape=shapes(((90,), jnp.int32), ((2, 4, 128, 256), BF16)),
        in_specs=[smem()] + [vmem()] * 2,
        out_specs=[smem(), vmem()],
        compiler_params=pltpu.CompilerParams(vmem_limit_bytes=24 * 1024 * 1024),
    )(active, pack, pack_other)
    rest = (bias, qd)
    state = stats_call((OWN,), True, False, lists, (own,), rest)
    state = stats_call((UP, DOWN), False, False, lists, (up, down), rest + (state,))
    stats = stats_call((UP2, DOWN2), False, True, lists, (up2, down2), rest + (state,))
    rest = rest + (stats,)
    (d_up2, d_down2), oq2 = back_call((UP2, DOWN2), lists, (up2, down2), rest)
    r_up2, r_down2 = to_z(d_up2, 2), to_z(d_down2, -2)
    (d_up,), oq1 = back_call((UP,), lists, (up,), rest)
    r_up = to_z(d_up, 1)
    (d_down,), oq3 = back_call((DOWN,), lists, (down,), rest)
    r_down = to_z(d_down, -1)
    (d_own,), oq0 = back_call((OWN,), lists, (own,), rest)
    oq = oq0 + oq1 + oq2 + oq3
    oq = jnp.concatenate([oq[:, :, :32] * SCALE, oq[:, :, 32:]], axis=2)
    oq_other = lax.ppermute(oq[1].astype(BF16), "xl", SWAP)
    out_keep, out_send = call(
        out_kernel, [((4, 64, 128), F32), ((4, 64, 128), BF16)], 0, 4
    )(oq, oq_other, gate, w_out)
    out_other = lax.ppermute(out_send, "c", SWAP)
    out = (out_keep + out_other.astype(F32)).astype(BF16)
    sums, sums_other = call(sum_kernel, [((4, 2, 128, 128), BF16)] * 2, 0, 5)(
        d_own, r_up, r_down, r_up2, r_down2
    )
    exchange = functools.partial(
        lax.all_to_all, axis_name="z", split_axis=0, concat_axis=0, axis_index_groups=groups, tiled=True
    )
    theirs = jnp.sum(exchange(sums_other).astype(F32), axis=0).astype(BF16)
    dkv_other = lax.ppermute(theirs, "xl", SWAP)
    dkv = exchange(sums)
    dkv, _, _ = lax.optimization_barrier((dkv, out_other, dkv_other))
    part, part_send = call(
        proj_kernel,
        [((4, 128, 128), F32), ((4, 128, 128), BF16)],
        0,
        7,
        [pltpu.VMEM((256, 128), F32)],
    )(oq, oq_other, dkv, dkv_other, gate, go, w_proj)
    (pair_gradient,) = call(final_kernel, [((4, 128, 128), BF16)], 0, 4)(
        pair, gain, part, lax.ppermute(part_send, "c", SWAP)
    )
    return jnp.swapaxes(out, 1, 2), pair_gradient


def solution(mesh):
    fine = Mesh(np.asarray(mesh.devices).reshape(2, 4, 2, 16, 2), ("xh", "y", "xl", "z", "c"))
    row, col = ("xh", "y"), ("xl", "z")
    return jax.shard_map(
        per_device,
        mesh=fine,
        in_specs=(
            P(row, col, None),
            P(),
            P(None, "c"),
            P("c", None),
            P("c", col, row),
            P(),
            P(row, col, None),
        ),
        out_specs=(P(row, col, "c"), P(row, col, None)),
        check_vma=False,
    )
```

```python
import functools

import jax
import jax.numpy as jnp
import numpy as np
from jax import lax
from jax.experimental import pallas as pl
from jax.experimental.pallas import tpu as pltpu
from jax.sharding import Mesh
from jax.sharding import PartitionSpec as P

DH = 32
SCALE = DH ** (-0.5)
EPS = 1e-05
NEG = -1e30
F32 = jnp.float32
BF16 = jnp.bfloat16
SWAP = [(0, 1), (1, 0)]
OWN, UP, DOWN, UP2, DOWN2 = range(5)
ARRAYS = ((0, 0, 4), (1, 0, 4), (-1, 0, 4), (2, 0, 2), (-2, 2, 2))


def place():
    return [lax.axis_index(name) for name in ("z", "xl", "c")]


def vmem():
    return pl.BlockSpec(memory_space=pltpu.VMEM)


def smem():
    return pl.BlockSpec(memory_space=pltpu.SMEM)


def shapes(*items):
    return [jax.ShapeDtypeStruct(s, d) for s, d in items]


def call(kernel, outs, n_smem, n_vmem, scratch=(), flops=0, nbytes=0):
    return pl.pallas_call(
        kernel,
        out_shape=shapes(*outs),
        in_specs=[smem()] * n_smem + [vmem()] * n_vmem,
        out_specs=[vmem()] * len(outs),
        scratch_shapes=list(scratch),
        compiler_params=pltpu.CompilerParams(vmem_limit_bytes=24 * 1024 * 1024),
        cost_estimate=pl.CostEstimate(flops=flops, bytes_accessed=nbytes, transcendentals=0),
    )


def nt(a, b):
    return lax.dot_general(a, b, (((1,), (1,)), ((), ())), preferred_element_type=F32)


def nn(a, b):
    return jnp.dot(a, b, preferred_element_type=F32)


def norm(x):
    mean = jnp.mean(x, axis=-1, keepdims=True)
    centred = x - mean
    inv = lax.rsqrt(jnp.mean(centred * centred, axis=-1, keepdims=True) + EPS)
    return centred * inv, inv


def prep_kernel(*refs):
    ids = place()
    here, (keep, send, gate_out, go_out, bias_out) = refs[:6], refs[6:11]
    pair, gain, w_proj, w_out, d_out, bias = local = refs[11:17]
    proj_s, sems = refs[17:]
    copies = [pltpu.make_async_copy(s, d, sems.at[k]) for k, (s, d) in enumerate(zip(here, local))]
    for copy in copies:
        copy.start()
    for copy in copies[:5]:
        copy.wait()
    xl = ids[1]
    w_t = w_proj[...].T
    for p in range(2):
        for i in range(2):
            r = 2 * p + i
            xhat, _ = norm(pair[r].astype(F32))
            normed = (xhat * gain[...]).astype(BF16)
            proj = nt(w_t, normed)
            go = nt(w_out[...], d_out[r])
            go_out[r] = go
            for h in range(2):
                gate = jax.nn.sigmoid(proj[h * 128 + 96 : h * 128 + 128])
                gate_out[r, h * DH : (h + 1) * DH] = gate
                proj_s[h, i * 64 : (i + 1) * 64] = proj[h * 128 + 32 : h * 128 + 96]
                proj_s[h, 128 + i * 64 : 160 + i * 64] = proj[h * 128 : h * 128 + 32] * SCALE
                proj_s[h, 160 + i * 64 : 192 + i * 64] = go[h * DH : (h + 1) * DH] * gate
        for ref, h in ((keep, xl), (send, 1 - xl)):
            ref[p * 128 : (p + 1) * 128] = proj_s[h, 0:128].T.astype(BF16)
            ref[256 + p * 128 : 384 + p * 128] = proj_s[h, 128:256].astype(BF16)
    copies[5].wait()
    for j in range(4):
        for h in range(2):
            block = bias[h, :, 128 * j : 128 * j + 128].T
            bias_out[h, j] = block
            bias_out[2 + h, j] = block


def fill_queries(qd, packs):
    qd[...] = jnp.zeros_like(qd)
    for half, pack in enumerate(packs):
        for r in range(4):
            low = 64 * (r % 2)
            qd[half, r, low : low + 32, 0:128] = pack[256 + 64 * r : 288 + 64 * r]
            qd[half, r, low + 32 : low + 64, 128:256] = pack[288 + 64 * r : 320 + 64 * r]


def tile_of(zk, xk):
    return zk // 2 + 8 * xk


def setup_kernel(act, pack0, pack1, lists, qd, kv):
    ids = place()
    for p in range(2):
        kv[0, p] = pack0[128 * p : 128 * p + 128]
        kv[1, p] = pack1[128 * p : 128 * p + 128]
    fill_queries(qd, (pack0, pack1))
    for k, (step, low, count) in enumerate(ARRAYS):
        for half in range(2):
            a = tile_of(ids[0], ids[1] if half == 0 else 1 - ids[1])
            base = 9 * (2 * k + half)
            n = 0
            for u in range(2 * count):
                zk = (ids[0] + step + 16) % 4 + 4 * (u // 2 + low)
                xk = ids[1] if u % 2 == 0 else 1 - ids[1]
                lists[base + n] = u
                n = n + act[a, tile_of(zk, xk)]
            lists[base + 8] = n


def load_units(ids, kv, bias, which, half, units):
    step, low, _ = ARRAYS[which]
    keys = [[kv[u // 2, u % 2, p] for u in units] for p in range(2)]
    b = []
    for u in units:
        xk = jnp.where(u % 2 == 0, ids[1], 1 - ids[1])
        xq = jnp.where(half == 0, ids[1], 1 - ids[1])
        b.append(bias[u // 2 + low, xk, xq, (ids[0] + step + 16) % 4].astype(F32))
    keys = [k[0] if len(k) == 1 else jnp.concatenate(k, axis=0) for k in keys]
    return keys, b[0] if len(b) == 1 else jnp.concatenate(b, axis=0)


def over_units(lists, which, half, body):
    base = 9 * (2 * which + half)
    n = lists[base + 8]

    @pl.loop(0, n // 2)
    def _(k):
        body([lists[base + 2 * k], lists[base + 2 * k + 1]])

    @pl.when(n % 2 == 1)
    def _():
        body([lists[base + n - 1]])


def stats_kernel(names, begin, end, lists, *refs):
    n, ids = len(names), place()
    kvs, (bias, qd), refs = refs[:n], refs[n : n + 2], refs[n + 2 :]
    before, refs = (None, refs) if begin else (refs[0], refs[1:])
    out, st = refs
    if begin:
        st[0] = jnp.full(st.shape[1:], NEG, F32)
        st[1:3] = jnp.zeros((2,) + st.shape[1:], F32)
    else:
        st[...] = before[...]

    @pl.loop(0, 2)
    def _(half):
        for kv, which in zip(kvs, names):

            def body(units, kv=kv, which=which):
                keys, b = load_units(ids, kv, bias, which, half, units)
                rows = b.shape[0] // 8
                for p in range(2):
                    sd = [nn(keys[p], qd[half, 2 * p + i]) for i in range(2)]
                    for i in range(2):
                        r = 2 * p + i
                        s = (sd[i][:, :128] + b).reshape(rows, 8, 128)
                        dp = sd[i][:, 128:].reshape(rows, 8, 128)
                        m_old = st[0, half, r]
                        m_new = jnp.maximum(m_old, jnp.max(s, axis=0))
                        e = jnp.exp(s - m_new[None])
                        c = jnp.exp(m_old - m_new)
                        st[1, half, r] = st[1, half, r] * c + jnp.sum(e, axis=0)
                        st[2, half, r] = st[2, half, r] * c + jnp.sum(e * dp, axis=0)
                        st[0, half, r] = m_new

            over_units(lists, which, half, body)

    if not end:
        out[...] = st[...]
        return
    for half in range(2):
        for r in range(4):
            m = st[0, half, r]
            top = jnp.max(m, axis=0, keepdims=True)
            f = jnp.exp(m - top)
            total = jnp.sum(st[1, half, r] * f, axis=0, keepdims=True)
            out[half, r, 0:1] = top + jnp.log(total)
            out[half, r, 1:2] = jnp.sum(st[2, half, r] * f, axis=0, keepdims=True) / total


def back_kernel(names, lists, *refs):
    n, ids = len(names), place()
    kvs, (bias, qd, stats) = refs[:n], refs[n : n + 3]
    dkvs, (oq, acc) = refs[n + 3 : 2 * n + 3], refs[2 * n + 3 :]
    oq[...] = jnp.zeros_like(oq)
    for kv, dkv, which in zip(kvs, dkvs, names):
        count = kv.shape[0]
        acc[0:count] = jnp.zeros((count,) + acc.shape[1:], F32)

        @pl.loop(0, 2)
        def _(half):
            def body(units):
                keys, b = load_units(ids, kv, bias, which, half, units)
                for p in range(2):
                    keys_t = keys[p].T
                    qs = [qd[half, 2 * p + i] for i in range(2)]
                    sd = [nn(keys[p], q) for q in qs]
                    pds = []
                    for i in range(2):
                        r = 2 * p + i
                        prob = jnp.exp(sd[i][:, :128] + (b - stats[half, r, 0:1]))
                        dsc = prob * (sd[i][:, 128:] - stats[half, r, 1:2])
                        pds.append(jnp.concatenate([dsc.astype(BF16), prob.astype(BF16)], axis=1))
                    both = nt(jnp.concatenate(pds, axis=1), jnp.concatenate(qs, axis=1))
                    for k, u in enumerate(units):
                        acc[u // 2, u % 2, p] += both[128 * k : 128 * k + 128]
                    for i in range(2):
                        r = 2 * p + i
                        t = nn(keys_t[64 * i : 64 * i + 64], pds[i])
                        oq[half, r, 0:32] += t[0:32, 0:128]
                        oq[half, r, 32:64] += t[32:64, 128:256]

            over_units(lists, which, half, body)

        dkv[...] = acc[0:count].astype(BF16)


def out_kernel(oq_own, oq_other, gate, w_out, keep, send):
    _, xl, c = place()
    w_t = w_out[...].T
    for r in range(4):
        mine, theirs = oq_own[0, r, 32:64], oq_other[r, 32:64].astype(F32)
        att = jnp.concatenate(
            [jnp.where(xl == 0, mine, theirs), jnp.where(xl == 0, theirs, mine)], axis=0
        )
        part = nn(w_t, (gate[r] * att).astype(BF16))
        low, high = part[0:64], part[64:128]
        keep[r] = jnp.where(c == 0, low, high)
        send[r] = jnp.where(c == 0, high, low).astype(BF16)


def sum_kernel(d_own, r_up, r_down, r_up2, r_down2, out):
    for m in range(4):
        total = d_own[m].astype(F32) + r_up[m].astype(F32) + r_down[m].astype(F32)
        total += (r_up2[m] if m < 2 else r_down2[m - 2]).astype(F32)
        out[m] = total.astype(BF16)


def proj_kernel(oq_own, oq_other, dkv_own, dkv_other, gate, go, w_proj, send, dp):
    _, xl, _ = place()
    for p in range(2):
        mine_kv = sum(dkv_own[m, 0, p].astype(F32) for m in range(4)).T
        theirs_kv = dkv_other[1 - xl, p].astype(F32).T
        for i in range(2):
            r = 2 * p + i
            for oq, kvt, h in (
                (oq_own[0, r], mine_kv, xl),
                (oq_other[r].astype(F32), theirs_kv, 1 - xl),
            ):
                low = pl.multiple_of(h * DH, DH)
                g = gate[r, pl.ds(low, DH)]
                base = pl.multiple_of(h * 128, 128)
                dp[pl.ds(base, 32)] = oq[0:32]
                dp[pl.ds(base + 32, 64)] = kvt[64 * i : 64 * i + 64]
                dp[pl.ds(base + 96, 32)] = go[r, pl.ds(low, DH)] * oq[32:64] * g * (1.0 - g)
            send[r] = nn(w_proj[...], dp[...].astype(BF16)).T.astype(BF16)


def final_kernel(pair, gain, parts, out):
    for r in range(4):
        xhat, inv = norm(pair[r].astype(F32))
        g = (parts[0, r].astype(F32) + parts[1, r].astype(F32)) * gain[...]
        mean = jnp.mean(g, axis=-1, keepdims=True)
        along = jnp.mean(g * xhat, axis=-1, keepdims=True)
        out[r] = (inv * (g - mean - xhat * along)).astype(BF16)


def stats_call(names, begin, end, lists, kvs, rest):
    out = ((2, 4, 2, 128), F32) if end else ((3, 2, 4, 8, 128), F32)
    return call(
        functools.partial(stats_kernel, names, begin, end),
        [out],
        1,
        len(kvs) + len(rest),
        [pltpu.VMEM((3, 2, 4, 8, 128), F32)],
        flops=10 ** 9,
        nbytes=10 ** 7,
    )(lists, *kvs, *rest)[0]


def back_call(names, lists, kvs, rest):
    res = call(
        functools.partial(back_kernel, names),
        [(kv.shape, BF16) for kv in kvs] + [((2, 4, 64, 128), F32)],
        1,
        len(kvs) + len(rest),
        [pltpu.VMEM((4, 2, 2, 128, 128), F32)],
        flops=2 * 10 ** 9,
        nbytes=2 * 10 ** 7,
    )(lists, *kvs, *rest)
    return res[:-1], res[-1]


def to_z(x, step):
    return lax.ppermute(x, "z", [(j, (j + step) % 16) for j in range(16)])


def per_device(pair, gain, w_proj, w_out, tri_bias, active, d_out):
    gain = gain.reshape(1, 128)
    args = (pair, gain, w_proj, w_out, d_out, tri_bias)
    pack, pack_send, gate, go, bias = pl.pallas_call(
        prep_kernel,
        out_shape=shapes(
            *[((512, 128), BF16)] * 2, *[((4, 64, 128), F32)] * 2, ((4, 4, 128, 128), BF16)
        ),
        in_specs=[pl.BlockSpec(memory_space=pl.ANY)] * 6,
        out_specs=[vmem()] * 5,
        scratch_shapes=[pltpu.VMEM(a.shape, a.dtype) for a in args]
        + [pltpu.VMEM((2, 256, 128), F32), pltpu.SemaphoreType.DMA((6,))],
        compiler_params=pltpu.CompilerParams(vmem_limit_bytes=56 * 1024 * 1024),
    )(*args)
    pack_other = lax.ppermute(pack_send, "xl", SWAP)
    bias = lax.all_to_all(bias, ("xh", "xl"), 0, 0, tiled=True).reshape(2, 2, 4, 128, 128)
    bias, pack_other = lax.optimization_barrier((bias, pack_other))
    bias = lax.all_gather(bias, "y")
    lists, qd, kv = pl.pallas_call(
        setup_kernel,
        out_shape=shapes(
            ((90,), jnp.int32), ((2, 4, 128, 256), BF16), ((2, 2, 128, 128), BF16)
        ),
        in_specs=[smem()] + [vmem()] * 2,
        out_specs=[smem(), vmem(), vmem()],
        compiler_params=pltpu.CompilerParams(vmem_limit_bytes=24 * 1024 * 1024),
    )(active, pack, pack_other)
    groups = [[k + 4 * m for m in range(4)] for k in range(4)]
    own = lax.all_gather(kv, "z", axis_index_groups=groups)
    up, down = to_z(own, -1), to_z(own, 1)
    up2, down2 = to_z(own[0:2], -2), to_z(own[2:4], 2)
    rest = (bias, qd)
    state = stats_call((OWN,), True, False, lists, (own,), rest)
    state = stats_call((UP, DOWN), False, False, lists, (up, down), rest + (state,))
    stats = stats_call((UP2, DOWN2), False, True, lists, (up2, down2), rest + (state,))
    rest = rest + (stats,)
    (d_up2, d_down2), oq2 = back_call((UP2, DOWN2), lists, (up2, down2), rest)
    r_up2, r_down2 = to_z(d_up2, 2), to_z(d_down2, -2)
    (d_up,), oq1 = back_call((UP,), lists, (up,), rest)
    r_up = to_z(d_up, 1)
    (d_down,), oq3 = back_call((DOWN,), lists, (down,), rest)
    r_down = to_z(d_down, -1)
    (d_own,), oq0 = back_call((OWN,), lists, (own,), rest)
    oq = oq0 + oq1 + oq2 + oq3
    oq = jnp.concatenate([oq[:, :, :32] * SCALE, oq[:, :, 32:]], axis=2)
    oq_other = lax.ppermute(oq[1].astype(BF16), "xl", SWAP)
    out_keep, out_send = call(
        out_kernel, [((4, 64, 128), F32), ((4, 64, 128), BF16)], 0, 4
    )(oq, oq_other, gate, w_out)
    out_other = lax.ppermute(out_send, "c", SWAP)
    out = (out_keep + out_other.astype(F32)).astype(BF16)
    (sums,) = call(sum_kernel, [((4, 2, 2, 128, 128), BF16)], 0, 5)(
        d_own, r_up, r_down, r_up2, r_down2
    )
    dkv = lax.all_to_all(sums, "z", 0, 0, axis_index_groups=groups, tiled=True)
    dkv, out = lax.optimization_barrier((dkv, out))
    theirs = jnp.sum(dkv[:, 1].astype(F32), axis=0).astype(BF16)
    (part,) = call(
        proj_kernel, [((4, 128, 128), BF16)], 0, 7, [pltpu.VMEM((256, 128), F32)]
    )(oq, oq_other, dkv, lax.all_gather(theirs, "xl"), gate, go, w_proj)
    (pair_gradient,) = call(final_kernel, [((4, 128, 128), BF16)], 0, 3)(
        pair, gain, lax.all_gather(part, "c")
    )
    return jnp.swapaxes(out, 1, 2), pair_gradient


def solution(mesh):
    fine = Mesh(np.asarray(mesh.devices).reshape(2, 4, 2, 16, 2), ("xh", "y", "xl", "z", "c"))
    row, col = ("xh", "y"), ("xl", "z")
    return jax.shard_map(
        per_device,
        mesh=fine,
        in_specs=(
            P(row, col, None),
            P(),
            P(None, "c"),
            P("c", None),
            P("c", col, row),
            P(),
            P(row, col, None),
        ),
        out_specs=(P(row, col, "c"), P(row, col, None)),
        check_vma=False,
    )
```

```python
import functools

import jax
import jax.numpy as jnp
import numpy as np
from jax import lax
from jax.experimental import pallas as pl
from jax.experimental.pallas import tpu as pltpu
from jax.sharding import Mesh
from jax.sharding import PartitionSpec as P

DH = 32
SCALE = DH ** (-0.5)
EPS = 1e-05
NEG = -1e30
F32 = jnp.float32
BF16 = jnp.bfloat16
SWAP = [(0, 1), (1, 0)]
OWN, UP, DOWN, UP2, DOWN2 = range(5)
ARRAYS = ((0, 0, 4), (1, 0, 4), (-1, 0, 4), (2, 0, 2), (-2, 2, 2))


def place():
    return [lax.axis_index(name) for name in ("z", "xl", "c")]


def vmem():
    return pl.BlockSpec(memory_space=pltpu.VMEM)


def smem():
    return pl.BlockSpec(memory_space=pltpu.SMEM)


def shapes(*items):
    return [jax.ShapeDtypeStruct(s, d) for s, d in items]


def call(kernel, outs, n_smem, n_vmem, scratch=(), flops=0, nbytes=0):
    return pl.pallas_call(
        kernel,
        out_shape=shapes(*outs),
        in_specs=[smem()] * n_smem + [vmem()] * n_vmem,
        out_specs=[vmem()] * len(outs),
        scratch_shapes=list(scratch),
        compiler_params=pltpu.CompilerParams(vmem_limit_bytes=24 * 1024 * 1024),
        cost_estimate=pl.CostEstimate(flops=flops, bytes_accessed=nbytes, transcendentals=0),
    )


def nt(a, b):
    return lax.dot_general(a, b, (((1,), (1,)), ((), ())), preferred_element_type=F32)


def nn(a, b):
    return jnp.dot(a, b, preferred_element_type=F32)


def norm(x):
    mean = jnp.mean(x, axis=-1, keepdims=True)
    centred = x - mean
    inv = lax.rsqrt(jnp.mean(centred * centred, axis=-1, keepdims=True) + EPS)
    return centred * inv, inv


def make_lists(ids, act, lists):
    for k, (step, low, count) in enumerate(ARRAYS):
        for half in range(2):
            a = tile_of(ids[0], ids[1] if half == 0 else 1 - ids[1])
            base = 9 * (2 * k + half)
            n = 0
            for u in range(2 * count):
                zk = (ids[0] + step + 16) % 4 + 4 * (u // 2 + low)
                xk = ids[1] if u % 2 == 0 else 1 - ids[1]
                lists[base + n] = u
                n = n + act[a, tile_of(zk, xk)]
            lists[base + 8] = n


def prep_kernel(*refs):
    ids = place()
    here, (keep, send, gate_out, go_out, bias_out, lists) = refs[:7], refs[7:13]
    pair, gain, w_proj, w_out, d_out, bias, act = local = refs[13:20]
    proj_s, sems = refs[20:]
    copies = [pltpu.make_async_copy(s, d, sems.at[k]) for k, (s, d) in enumerate(zip(here, local))]
    for copy in reversed(copies):
        copy.start()
    copies[6].wait()
    make_lists(ids, act, lists)
    for copy in copies[:5]:
        copy.wait()
    xl = ids[1]
    w_t = w_proj[...].T
    for p in range(2):
        for i in range(2):
            r = 2 * p + i
            xhat, _ = norm(pair[r].astype(F32))
            normed = (xhat * gain[...]).astype(BF16)
            proj = nt(w_t, normed)
            go = nt(w_out[...], d_out[r])
            go_out[r] = go
            for h in range(2):
                gate = jax.nn.sigmoid(proj[h * 128 + 96 : h * 128 + 128])
                gate_out[r, h * DH : (h + 1) * DH] = gate
                proj_s[h, i * 64 : (i + 1) * 64] = proj[h * 128 + 32 : h * 128 + 96]
                proj_s[h, 128 + i * 64 : 160 + i * 64] = proj[h * 128 : h * 128 + 32] * SCALE
                proj_s[h, 160 + i * 64 : 192 + i * 64] = go[h * DH : (h + 1) * DH] * gate
        for ref, h in ((keep, xl), (send, 1 - xl)):
            ref[p * 128 : (p + 1) * 128] = proj_s[h, 0:128].T.astype(BF16)
            ref[256 + p * 128 : 384 + p * 128] = proj_s[h, 128:256].astype(BF16)
    copies[5].wait()
    for j in range(4):
        for h in range(2):
            block = bias[h, :, 128 * j : 128 * j + 128].T
            bias_out[h, j] = block
            bias_out[2 + h, j] = block


def fill_queries(qd, packs):
    qd[...] = jnp.zeros_like(qd)
    for half, pack in enumerate(packs):
        for r in range(4):
            low = 64 * (r % 2)
            qd[half, r, low : low + 32, 0:128] = pack[256 + 64 * r : 288 + 64 * r]
            qd[half, r, low + 32 : low + 64, 128:256] = pack[288 + 64 * r : 320 + 64 * r]


def tile_of(zk, xk):
    return zk // 2 + 8 * xk


def setup_kernel(pack0, pack1, qd, kv):
    for p in range(2):
        kv[0, p] = pack0[128 * p : 128 * p + 128]
        kv[1, p] = pack1[128 * p : 128 * p + 128]
    fill_queries(qd, (pack0, pack1))


def load_units(ids, kv, bias, which, half, units):
    step, low, _ = ARRAYS[which]
    keys = [[kv[u // 2, u % 2, p] for u in units] for p in range(2)]
    b = []
    for u in units:
        xk = jnp.where(u % 2 == 0, ids[1], 1 - ids[1])
        xq = jnp.where(half == 0, ids[1], 1 - ids[1])
        b.append(bias[u // 2 + low, xk, xq, (ids[0] + step + 16) % 4].astype(F32))
    keys = [k[0] if len(k) == 1 else jnp.concatenate(k, axis=0) for k in keys]
    return keys, b[0] if len(b) == 1 else jnp.concatenate(b, axis=0)


def over_units(lists, which, half, body):
    base = 9 * (2 * which + half)
    n = lists[base + 8]

    @pl.loop(0, n // 2)
    def _(k):
        body([lists[base + 2 * k], lists[base + 2 * k + 1]])

    @pl.when(n % 2 == 1)
    def _():
        body([lists[base + n - 1]])


def stats_kernel(names, begin, end, lists, *refs):
    n, ids = len(names), place()
    kvs, (bias, qd), refs = refs[:n], refs[n : n + 2], refs[n + 2 :]
    before, refs = (None, refs) if begin else (refs[0], refs[1:])
    out, st = refs
    if begin:
        st[0] = jnp.full(st.shape[1:], NEG, F32)
        st[1:3] = jnp.zeros((2,) + st.shape[1:], F32)
    else:
        st[...] = before[...]

    @pl.loop(0, 2)
    def _(half):
        for kv, which in zip(kvs, names):

            def body(units, kv=kv, which=which):
                keys, b = load_units(ids, kv, bias, which, half, units)
                rows = b.shape[0] // 8
                for p in range(2):
                    sd = [nn(keys[p], qd[half, 2 * p + i]) for i in range(2)]
                    for i in range(2):
                        r = 2 * p + i
                        s = (sd[i][:, :128] + b).reshape(rows, 8, 128)
                        dp = sd[i][:, 128:].reshape(rows, 8, 128)
                        m_old = st[0, half, r]
                        m_new = jnp.maximum(m_old, jnp.max(s, axis=0))
                        e = jnp.exp(s - m_new[None])
                        c = jnp.exp(m_old - m_new)
                        st[1, half, r] = st[1, half, r] * c + jnp.sum(e, axis=0)
                        st[2, half, r] = st[2, half, r] * c + jnp.sum(e * dp, axis=0)
                        st[0, half, r] = m_new

            over_units(lists, which, half, body)

    if not end:
        out[...] = st[...]
        return
    for half in range(2):
        for r in range(4):
            m = st[0, half, r]
            top = jnp.max(m, axis=0, keepdims=True)
            f = jnp.exp(m - top)
            total = jnp.sum(st[1, half, r] * f, axis=0, keepdims=True)
            out[half, r, 0:1] = top + jnp.log(total)
            out[half, r, 1:2] = jnp.sum(st[2, half, r] * f, axis=0, keepdims=True) / total


def back_kernel(names, lists, *refs):
    n, ids = len(names), place()
    kvs, (bias, qd, stats) = refs[:n], refs[n : n + 3]
    dkvs, (oq, acc) = refs[n + 3 : 2 * n + 3], refs[2 * n + 3 :]
    oq[...] = jnp.zeros_like(oq)
    for kv, dkv, which in zip(kvs, dkvs, names):
        count = kv.shape[0]
        acc[0:count] = jnp.zeros((count,) + acc.shape[1:], F32)

        @pl.loop(0, 2)
        def _(half):
            def body(units):
                keys, b = load_units(ids, kv, bias, which, half, units)
                for p in range(2):
                    keys_t = keys[p].T
                    qs = [qd[half, 2 * p + i] for i in range(2)]
                    sd = [nn(keys[p], q) for q in qs]
                    pds = []
                    for i in range(2):
                        r = 2 * p + i
                        prob = jnp.exp(sd[i][:, :128] + (b - stats[half, r, 0:1]))
                        dsc = prob * (sd[i][:, 128:] - stats[half, r, 1:2])
                        pds.append(jnp.concatenate([dsc.astype(BF16), prob.astype(BF16)], axis=1))
                    both = nt(jnp.concatenate(pds, axis=1), jnp.concatenate(qs, axis=1))
                    for k, u in enumerate(units):
                        acc[u // 2, u % 2, p] += both[128 * k : 128 * k + 128]
                    for i in range(2):
                        r = 2 * p + i
                        t = nn(keys_t[64 * i : 64 * i + 64], pds[i])
                        oq[half, r, 0:32] += t[0:32, 0:128]
                        oq[half, r, 32:64] += t[32:64, 128:256]

            over_units(lists, which, half, body)

        dkv[...] = acc[0:count].astype(BF16)


def mid_kernel(lists, up2, down2, up, down, bias, qd, before, stats, d_up, d_down, oq, st, acc):
    stats_kernel((UP2, DOWN2), False, True, lists, up2, down2, bias, qd, before, stats, st)
    back_kernel((UP, DOWN), lists, up, down, bias, qd, stats, d_up, d_down, oq, acc)


def out_kernel(oq_own, oq_other, gate, w_out, keep, send):
    _, xl, c = place()
    w_t = w_out[...].T
    for r in range(4):
        mine, theirs = oq_own[0, r, 32:64], oq_other[r, 32:64].astype(F32)
        att = jnp.concatenate(
            [jnp.where(xl == 0, mine, theirs), jnp.where(xl == 0, theirs, mine)], axis=0
        )
        part = nn(w_t, (gate[r] * att).astype(BF16))
        low, high = part[0:64], part[64:128]
        keep[r] = jnp.where(c == 0, low, high)
        send[r] = jnp.where(c == 0, high, low).astype(BF16)


def sum_kernel(d_own, r_up, r_down, r_up2, r_down2, out):
    for m in range(4):
        total = d_own[m].astype(F32) + r_up[m].astype(F32) + r_down[m].astype(F32)
        total += (r_up2[m] if m < 2 else r_down2[m - 2]).astype(F32)
        out[m] = total.astype(BF16)


def proj_kernel(oq_own, oq_other, dkv_own, dkv_other, gate, go, w_proj, send, dp):
    _, xl, _ = place()
    for p in range(2):
        mine_kv = sum(dkv_own[m, 0, p].astype(F32) for m in range(4)).T
        theirs_kv = dkv_other[1 - xl, p].astype(F32).T
        for i in range(2):
            r = 2 * p + i
            for oq, kvt, h in (
                (oq_own[0, r], mine_kv, xl),
                (oq_other[r].astype(F32), theirs_kv, 1 - xl),
            ):
                low = pl.multiple_of(h * DH, DH)
                g = gate[r, pl.ds(low, DH)]
                base = pl.multiple_of(h * 128, 128)
                dp[pl.ds(base, 32)] = oq[0:32]
                dp[pl.ds(base + 32, 64)] = kvt[64 * i : 64 * i + 64]
                dp[pl.ds(base + 96, 32)] = go[r, pl.ds(low, DH)] * oq[32:64] * g * (1.0 - g)
            send[r] = nn(w_proj[...], dp[...].astype(BF16)).T.astype(BF16)


def final_kernel(pair, gain, parts, out):
    for r in range(4):
        xhat, inv = norm(pair[r].astype(F32))
        g = (parts[0, r].astype(F32) + parts[1, r].astype(F32)) * gain[...]
        mean = jnp.mean(g, axis=-1, keepdims=True)
        along = jnp.mean(g * xhat, axis=-1, keepdims=True)
        out[r] = (inv * (g - mean - xhat * along)).astype(BF16)


def stats_call(names, begin, end, lists, kvs, rest):
    out = ((2, 4, 2, 128), F32) if end else ((3, 2, 4, 8, 128), F32)
    return call(
        functools.partial(stats_kernel, names, begin, end),
        [out],
        1,
        len(kvs) + len(rest),
        [pltpu.VMEM((3, 2, 4, 8, 128), F32)],
        flops=10 ** 9,
        nbytes=10 ** 7,
    )(lists, *kvs, *rest)[0]


def back_call(names, lists, kvs, rest):
    res = call(
        functools.partial(back_kernel, names),
        [(kv.shape, BF16) for kv in kvs] + [((2, 4, 64, 128), F32)],
        1,
        len(kvs) + len(rest),
        [pltpu.VMEM((4, 2, 2, 128, 128), F32)],
        flops=2 * 10 ** 9,
        nbytes=2 * 10 ** 7,
    )(lists, *kvs, *rest)
    return res[:-1], res[-1]


def to_z(x, step):
    return lax.ppermute(x, "z", [(j, (j + step) % 16) for j in range(16)])


def per_device(pair, gain, w_proj, w_out, tri_bias, active, d_out):
    gain = gain.reshape(1, 128)
    args = (pair, gain, w_proj, w_out, d_out, tri_bias, active)
    pack, pack_send, gate, go, bias, lists = pl.pallas_call(
        prep_kernel,
        out_shape=shapes(
            *[((512, 128), BF16)] * 2, *[((4, 64, 128), F32)] * 2, ((4, 4, 128, 128), BF16),
            ((90,), jnp.int32),
        ),
        in_specs=[pl.BlockSpec(memory_space=pl.ANY)] * 7,
        out_specs=[vmem()] * 5 + [smem()],
        scratch_shapes=[pltpu.VMEM(a.shape, a.dtype) for a in args[:6]]
        + [pltpu.SMEM(active.shape, active.dtype)]
        + [pltpu.VMEM((2, 256, 128), F32), pltpu.SemaphoreType.DMA((7,))],
        compiler_params=pltpu.CompilerParams(vmem_limit_bytes=56 * 1024 * 1024),
    )(*args)
    pack_other = lax.ppermute(pack_send, "xl", SWAP)
    bias = lax.all_to_all(bias, ("xh", "xl"), 0, 0, tiled=True).reshape(2, 2, 4, 128, 128)
    bias, pack_other = lax.optimization_barrier((bias, pack_other))
    bias = lax.all_gather(bias, "y")
    qd, kv = call(
        setup_kernel, [((2, 4, 128, 256), BF16), ((2, 2, 128, 128), BF16)], 0, 2
    )(pack, pack_other)
    groups = [[k + 4 * m for m in range(4)] for k in range(4)]
    own = lax.all_gather(kv, "z", axis_index_groups=groups)
    up, down = to_z(own, -1), to_z(own, 1)
    up2, down2 = to_z(own[0:2], -2), to_z(own[2:4], 2)
    rest = (bias, qd)
    state = stats_call((OWN,), True, False, lists, (own,), rest)
    state = stats_call((UP, DOWN), False, False, lists, (up, down), rest + (state,))
    stats, d_up, d_down, oq1 = call(
        mid_kernel,
        [((2, 4, 2, 128), F32), (up.shape, BF16), (down.shape, BF16), ((2, 4, 64, 128), F32)],
        1,
        7,
        [pltpu.VMEM((3, 2, 4, 8, 128), F32), pltpu.VMEM((4, 2, 2, 128, 128), F32)],
        flops=3 * 10 ** 9,
        nbytes=3 * 10 ** 7,
    )(lists, up2, down2, up, down, bias, qd, state)
    r_up, r_down = to_z(d_up, 1), to_z(d_down, -1)
    rest = rest + (stats,)
    (d_up2, d_down2), oq2 = back_call((UP2, DOWN2), lists, (up2, down2), rest)
    r_up2, r_down2 = to_z(d_up2, 2), to_z(d_down2, -2)
    (d_own,), oq0 = back_call((OWN,), lists, (own,), rest)
    oq = oq0 + oq1 + oq2
    oq = jnp.concatenate([oq[:, :, :32] * SCALE, oq[:, :, 32:]], axis=2)
    oq_other = lax.ppermute(oq[1].astype(BF16), "xl", SWAP)
    out_keep, out_send = call(
        out_kernel, [((4, 64, 128), F32), ((4, 64, 128), BF16)], 0, 4
    )(oq, oq_other, gate, w_out)
    out_other = lax.ppermute(out_send, "c", SWAP)
    out = (out_keep + out_other.astype(F32)).astype(BF16)
    (sums,) = call(sum_kernel, [((4, 2, 2, 128, 128), BF16)], 0, 5)(
        d_own, r_up, r_down, r_up2, r_down2
    )
    dkv = lax.all_to_all(sums, "z", 0, 0, axis_index_groups=groups, tiled=True)
    dkv, out = lax.optimization_barrier((dkv, out))
    theirs = jnp.sum(dkv[:, 1].astype(F32), axis=0).astype(BF16)
    (part,) = call(
        proj_kernel, [((4, 128, 128), BF16)], 0, 7, [pltpu.VMEM((256, 128), F32)]
    )(oq, oq_other, dkv, lax.all_gather(theirs, "xl"), gate, go, w_proj)
    (pair_gradient,) = call(final_kernel, [((4, 128, 128), BF16)], 0, 3)(
        pair, gain, lax.all_gather(part, "c")
    )
    return jnp.swapaxes(out, 1, 2), pair_gradient


def solution(mesh):
    fine = Mesh(np.asarray(mesh.devices).reshape(2, 4, 2, 16, 2), ("xh", "y", "xl", "z", "c"))
    row, col = ("xh", "y"), ("xl", "z")
    return jax.shard_map(
        per_device,
        mesh=fine,
        in_specs=(
            P(row, col, None),
            P(),
            P(None, "c"),
            P("c", None),
            P("c", col, row),
            P(),
            P(row, col, None),
        ),
        out_specs=(P(row, col, "c"), P(row, col, None)),
        check_vma=False,
    )
```

```python
import functools

import jax
import jax.numpy as jnp
import numpy as np
from jax import lax
from jax.experimental import pallas as pl
from jax.experimental.pallas import tpu as pltpu
from jax.sharding import Mesh
from jax.sharding import PartitionSpec as P

DH = 32
SCALE = DH ** (-0.5)
EPS = 1e-05
NEG = -1e30
F32 = jnp.float32
BF16 = jnp.bfloat16
SWAP = [(0, 1), (1, 0)]
OWN, UP, DOWN, UP2, DOWN2 = range(5)
ARRAYS = ((0, 0, 4), (1, 0, 4), (-1, 0, 4), (2, 0, 2), (-2, 2, 2))


def place():
    return [lax.axis_index(name) for name in ("z", "xl", "c")]


def vmem():
    return pl.BlockSpec(memory_space=pltpu.VMEM)


def smem():
    return pl.BlockSpec(memory_space=pltpu.SMEM)


def shapes(*items):
    return [jax.ShapeDtypeStruct(s, d) for s, d in items]


def call(kernel, outs, n_smem, n_vmem, scratch=(), flops=0, nbytes=0):
    return pl.pallas_call(
        kernel,
        out_shape=shapes(*outs),
        in_specs=[smem()] * n_smem + [vmem()] * n_vmem,
        out_specs=[vmem()] * len(outs),
        scratch_shapes=list(scratch),
        compiler_params=pltpu.CompilerParams(vmem_limit_bytes=24 * 1024 * 1024),
        cost_estimate=pl.CostEstimate(flops=flops, bytes_accessed=nbytes, transcendentals=0),
    )


def nt(a, b):
    return lax.dot_general(a, b, (((1,), (1,)), ((), ())), preferred_element_type=F32)


def nn(a, b):
    return jnp.dot(a, b, preferred_element_type=F32)


def norm(x):
    mean = jnp.mean(x, axis=-1, keepdims=True)
    centred = x - mean
    inv = lax.rsqrt(jnp.mean(centred * centred, axis=-1, keepdims=True) + EPS)
    return centred * inv, inv


def make_lists(ids, act, lists):
    for k, (step, low, count) in enumerate(ARRAYS):
        for half in range(2):
            a = tile_of(ids[0], ids[1] if half == 0 else 1 - ids[1])
            base = 9 * (2 * k + half)
            n = 0
            for u in range(2 * count):
                zk = (ids[0] + step + 16) % 4 + 4 * (u // 2 + low)
                xk = ids[1] if u % 2 == 0 else 1 - ids[1]
                lists[base + n] = u
                n = n + act[a, tile_of(zk, xk)]
            lists[base + 8] = n


def prep_kernel(*refs):
    ids = place()
    here, (keep, send, gate_out, go_out, bias_out, lists) = refs[:7], refs[7:13]
    pair, gain, w_proj, w_out, d_out, bias, act = local = refs[13:20]
    proj_s, sems = refs[20:]
    copies = [pltpu.make_async_copy(s, d, sems.at[k]) for k, (s, d) in enumerate(zip(here, local))]
    for copy in reversed(copies):
        copy.start()
    copies[6].wait()
    make_lists(ids, act, lists)
    for copy in copies[:5]:
        copy.wait()
    xl = ids[1]
    w_t = w_proj[...].T
    for p in range(2):
        for i in range(2):
            r = 2 * p + i
            xhat, _ = norm(pair[r].astype(F32))
            normed = (xhat * gain[...]).astype(BF16)
            proj = nt(w_t, normed)
            go = nt(w_out[...], d_out[r])
            go_out[r] = go
            for h in range(2):
                gate = jax.nn.sigmoid(proj[h * 128 + 96 : h * 128 + 128])
                gate_out[r, h * DH : (h + 1) * DH] = gate
                proj_s[h, i * 64 : (i + 1) * 64] = proj[h * 128 + 32 : h * 128 + 96]
                proj_s[h, 128 + i * 64 : 160 + i * 64] = proj[h * 128 : h * 128 + 32] * SCALE
                proj_s[h, 160 + i * 64 : 192 + i * 64] = go[h * DH : (h + 1) * DH] * gate
        for ref, h in ((keep, xl), (send, 1 - xl)):
            ref[p * 128 : (p + 1) * 128] = proj_s[h, 0:128].T.astype(BF16)
            ref[256 + p * 128 : 384 + p * 128] = proj_s[h, 128:256].astype(BF16)
    copies[5].wait()
    for j in range(4):
        for h in range(2):
            block = bias[h, :, 128 * j : 128 * j + 128].T
            bias_out[h, j] = block
            bias_out[2 + h, j] = block


def fill_queries(qd, packs):
    qd[...] = jnp.zeros_like(qd)
    for half, pack in enumerate(packs):
        for r in range(4):
            low = 64 * (r % 2)
            qd[half, r, low : low + 32, 0:128] = pack[256 + 64 * r : 288 + 64 * r]
            qd[half, r, low + 32 : low + 64, 128:256] = pack[288 + 64 * r : 320 + 64 * r]


def tile_of(zk, xk):
    return zk // 2 + 8 * xk


def setup_kernel(pack0, pack1, qd, kv):
    for p in range(2):
        kv[0, p] = pack0[128 * p : 128 * p + 128]
        kv[1, p] = pack1[128 * p : 128 * p + 128]
    fill_queries(qd, (pack0, pack1))


def load_units(ids, kv, bias, which, half, units):
    step, low, _ = ARRAYS[which]
    keys = [[kv[u // 2, u % 2, p] for u in units] for p in range(2)]
    b = []
    for u in units:
        xk = jnp.where(u % 2 == 0, ids[1], 1 - ids[1])
        xq = jnp.where(half == 0, ids[1], 1 - ids[1])
        b.append(bias[u // 2 + low, xk, xq, (ids[0] + step + 16) % 4].astype(F32))
    keys = [k[0] if len(k) == 1 else jnp.concatenate(k, axis=0) for k in keys]
    return keys, b[0] if len(b) == 1 else jnp.concatenate(b, axis=0)


def over_units(lists, which, half, body):
    base = 9 * (2 * which + half)
    n = lists[base + 8]

    @pl.loop(0, n // 4)
    def _(k):
        body([lists[base + 4 * k + j] for j in range(4)])

    @pl.when(n % 4 >= 2)
    def _():
        body([lists[base + n // 4 * 4], lists[base + n // 4 * 4 + 1]])

    @pl.when(n % 2 == 1)
    def _():
        body([lists[base + n - 1]])


def stats_kernel(names, begin, end, lists, *refs):
    n, ids = len(names), place()
    kvs, (bias, qd), refs = refs[:n], refs[n : n + 2], refs[n + 2 :]
    before, refs = (None, refs) if begin else (refs[0], refs[1:])
    out, st = refs
    if begin:
        st[0] = jnp.full(st.shape[1:], NEG, F32)
        st[1:3] = jnp.zeros((2,) + st.shape[1:], F32)
    else:
        st[...] = before[...]

    @pl.loop(0, 2)
    def _(half):
        for kv, which in zip(kvs, names):

            def body(units, kv=kv, which=which):
                keys, b = load_units(ids, kv, bias, which, half, units)
                for r in range(4):
                    sd = nn(keys[r // 2], qd[half, r])
                    m, l, d = (st[k, half, r] for k in range(3))
                    for low in range(0, b.shape[0], 64):
                        rows = slice(low, low + 64)
                        s = (sd[rows, :128] + b[rows]).reshape(-1, 8, 128)
                        dp = sd[rows, 128:].reshape(-1, 8, 128)
                        m_new = jnp.maximum(m, jnp.max(s, axis=0))
                        e = jnp.exp(s - m_new[None])
                        c = jnp.exp(m - m_new)
                        m, l, d = m_new, l * c + jnp.sum(e, axis=0), d * c + jnp.sum(e * dp, axis=0)
                    st[0, half, r], st[1, half, r], st[2, half, r] = m, l, d

            over_units(lists, which, half, body)

    if not end:
        out[...] = st[...]
        return
    for half in range(2):
        for r in range(4):
            m = st[0, half, r]
            top = jnp.max(m, axis=0, keepdims=True)
            f = jnp.exp(m - top)
            total = jnp.sum(st[1, half, r] * f, axis=0, keepdims=True)
            out[half, r, 0:1] = top + jnp.log(total)
            out[half, r, 1:2] = jnp.sum(st[2, half, r] * f, axis=0, keepdims=True) / total


def back_kernel(names, lists, *refs):
    n, ids = len(names), place()
    kvs, (bias, qd, stats) = refs[:n], refs[n : n + 3]
    dkvs, (oq, acc) = refs[n + 3 : 2 * n + 3], refs[2 * n + 3 :]
    oq[...] = jnp.zeros_like(oq)
    for kv, dkv, which in zip(kvs, dkvs, names):
        count = kv.shape[0]
        acc[0:count] = jnp.zeros((count,) + acc.shape[1:], F32)

        @pl.loop(0, 2)
        def _(half):
            def body(units):
                keys, b = load_units(ids, kv, bias, which, half, units)
                for p in range(2):
                    keys_t = keys[p].T
                    qs = [qd[half, 2 * p + i] for i in range(2)]
                    sd = [nn(keys[p], q) for q in qs]
                    pds = []
                    for i in range(2):
                        r = 2 * p + i
                        prob = jnp.exp(sd[i][:, :128] + (b - stats[half, r, 0:1]))
                        dsc = prob * (sd[i][:, 128:] - stats[half, r, 1:2])
                        pds.append(jnp.concatenate([dsc.astype(BF16), prob.astype(BF16)], axis=1))
                    both = nt(jnp.concatenate(pds, axis=1), jnp.concatenate(qs, axis=1))
                    for k, u in enumerate(units):
                        acc[u // 2, u % 2, p] += both[128 * k : 128 * k + 128]
                    for i in range(2):
                        r = 2 * p + i
                        t = nn(keys_t[64 * i : 64 * i + 64], pds[i])
                        oq[half, r, 0:32] += t[0:32, 0:128]
                        oq[half, r, 32:64] += t[32:64, 128:256]

            over_units(lists, which, half, body)

        dkv[...] = acc[0:count].astype(BF16)


def mid_kernel(lists, up2, down2, up, down, bias, qd, before, stats, d_up, d_down, oq, st, acc):
    stats_kernel((UP2, DOWN2), False, True, lists, up2, down2, bias, qd, before, stats, st)
    back_kernel((UP, DOWN), lists, up, down, bias, qd, stats, d_up, d_down, oq, acc)


def out_kernel(oq_own, oq_other, gate, w_out, keep, send):
    _, xl, c = place()
    w_t = w_out[...].T
    for r in range(4):
        mine, theirs = oq_own[0, r, 32:64], oq_other[r, 32:64].astype(F32)
        att = jnp.concatenate(
            [jnp.where(xl == 0, mine, theirs), jnp.where(xl == 0, theirs, mine)], axis=0
        )
        part = nn(w_t, (gate[r] * att).astype(BF16))
        low, high = part[0:64], part[64:128]
        keep[r] = jnp.where(c == 0, low, high)
        send[r] = jnp.where(c == 0, high, low).astype(BF16)


def sum_kernel(d_own, r_up, r_down, r_up2, r_down2, out):
    for m in range(4):
        total = d_own[m].astype(F32) + r_up[m].astype(F32) + r_down[m].astype(F32)
        total += (r_up2[m] if m < 2 else r_down2[m - 2]).astype(F32)
        out[m] = total.astype(BF16)


def proj_kernel(oq_own, oq_other, dkv_own, dkv_other, gate, go, w_proj, send, dp):
    _, xl, _ = place()
    for p in range(2):
        mine_kv = sum(dkv_own[m, 0, p].astype(F32) for m in range(4)).T
        theirs_kv = dkv_other[1 - xl, p].astype(F32).T
        for i in range(2):
            r = 2 * p + i
            for oq, kvt, h in (
                (oq_own[0, r], mine_kv, xl),
                (oq_other[r].astype(F32), theirs_kv, 1 - xl),
            ):
                low = pl.multiple_of(h * DH, DH)
                g = gate[r, pl.ds(low, DH)]
                base = pl.multiple_of(h * 128, 128)
                dp[pl.ds(base, 32)] = oq[0:32]
                dp[pl.ds(base + 32, 64)] = kvt[64 * i : 64 * i + 64]
                dp[pl.ds(base + 96, 32)] = go[r, pl.ds(low, DH)] * oq[32:64] * g * (1.0 - g)
            send[r] = nn(w_proj[...], dp[...].astype(BF16)).T.astype(BF16)


def final_kernel(pair, gain, parts, out):
    for r in range(4):
        xhat, inv = norm(pair[r].astype(F32))
        g = (parts[0, r].astype(F32) + parts[1, r].astype(F32)) * gain[...]
        mean = jnp.mean(g, axis=-1, keepdims=True)
        along = jnp.mean(g * xhat, axis=-1, keepdims=True)
        out[r] = (inv * (g - mean - xhat * along)).astype(BF16)


def stats_call(names, begin, end, lists, kvs, rest):
    out = ((2, 4, 2, 128), F32) if end else ((3, 2, 4, 8, 128), F32)
    return call(
        functools.partial(stats_kernel, names, begin, end),
        [out],
        1,
        len(kvs) + len(rest),
        [pltpu.VMEM((3, 2, 4, 8, 128), F32)],
        flops=10 ** 9,
        nbytes=10 ** 7,
    )(lists, *kvs, *rest)[0]


def back_call(names, lists, kvs, rest):
    res = call(
        functools.partial(back_kernel, names),
        [(kv.shape, BF16) for kv in kvs] + [((2, 4, 64, 128), F32)],
        1,
        len(kvs) + len(rest),
        [pltpu.VMEM((4, 2, 2, 128, 128), F32)],
        flops=2 * 10 ** 9,
        nbytes=2 * 10 ** 7,
    )(lists, *kvs, *rest)
    return res[:-1], res[-1]


def to_z(x, step):
    return lax.ppermute(x, "z", [(j, (j + step) % 16) for j in range(16)])


def per_device(pair, gain, w_proj, w_out, tri_bias, active, d_out):
    gain = gain.reshape(1, 128)
    args = (pair, gain, w_proj, w_out, d_out, tri_bias, active)
    pack, pack_send, gate, go, bias, lists = pl.pallas_call(
        prep_kernel,
        out_shape=shapes(
            *[((512, 128), BF16)] * 2, *[((4, 64, 128), F32)] * 2, ((4, 4, 128, 128), BF16),
            ((90,), jnp.int32),
        ),
        in_specs=[pl.BlockSpec(memory_space=pl.ANY)] * 7,
        out_specs=[vmem()] * 5 + [smem()],
        scratch_shapes=[pltpu.VMEM(a.shape, a.dtype) for a in args[:6]]
        + [pltpu.SMEM(active.shape, active.dtype)]
        + [pltpu.VMEM((2, 256, 128), F32), pltpu.SemaphoreType.DMA((7,))],
        compiler_params=pltpu.CompilerParams(vmem_limit_bytes=56 * 1024 * 1024),
    )(*args)
    pack_other = lax.ppermute(pack_send, "xl", SWAP)
    bias = lax.all_to_all(bias, ("xh", "xl"), 0, 0, tiled=True).reshape(2, 2, 4, 128, 128)
    bias, pack_other = lax.optimization_barrier((bias, pack_other))
    bias = lax.all_gather(bias, "y")
    qd, kv = call(
        setup_kernel, [((2, 4, 128, 256), BF16), ((2, 2, 128, 128), BF16)], 0, 2
    )(pack, pack_other)
    groups = [[k + 4 * m for m in range(4)] for k in range(4)]
    own = lax.all_gather(kv, "z", axis_index_groups=groups)
    up, down = to_z(own, -1), to_z(own, 1)
    up2, down2 = to_z(own[0:2], -2), to_z(own[2:4], 2)
    rest = (bias, qd)
    state = stats_call((OWN,), True, False, lists, (own,), rest)
    state = stats_call((UP, DOWN), False, False, lists, (up, down), rest + (state,))
    stats, d_up, d_down, oq1 = call(
        mid_kernel,
        [((2, 4, 2, 128), F32), (up.shape, BF16), (down.shape, BF16), ((2, 4, 64, 128), F32)],
        1,
        7,
        [pltpu.VMEM((3, 2, 4, 8, 128), F32), pltpu.VMEM((4, 2, 2, 128, 128), F32)],
        flops=3 * 10 ** 9,
        nbytes=3 * 10 ** 7,
    )(lists, up2, down2, up, down, bias, qd, state)
    r_up, r_down = to_z(d_up, 1), to_z(d_down, -1)
    rest = rest + (stats,)
    (d_up2, d_down2), oq2 = back_call((UP2, DOWN2), lists, (up2, down2), rest)
    r_up2, r_down2 = to_z(d_up2, 2), to_z(d_down2, -2)
    (d_own,), oq0 = back_call((OWN,), lists, (own,), rest)
    oq = oq0 + oq1 + oq2
    oq = jnp.concatenate([oq[:, :, :32] * SCALE, oq[:, :, 32:]], axis=2)
    oq_other = lax.ppermute(oq[1].astype(BF16), "xl", SWAP)
    out_keep, out_send = call(
        out_kernel, [((4, 64, 128), F32), ((4, 64, 128), BF16)], 0, 4
    )(oq, oq_other, gate, w_out)
    out_other = lax.ppermute(out_send, "c", SWAP)
    out = (out_keep + out_other.astype(F32)).astype(BF16)
    (sums,) = call(sum_kernel, [((4, 2, 2, 128, 128), BF16)], 0, 5)(
        d_own, r_up, r_down, r_up2, r_down2
    )
    dkv = lax.all_to_all(sums, "z", 0, 0, axis_index_groups=groups, tiled=True)
    dkv, out = lax.optimization_barrier((dkv, out))
    theirs = jnp.sum(dkv[:, 1].astype(F32), axis=0).astype(BF16)
    (part,) = call(
        proj_kernel, [((4, 128, 128), BF16)], 0, 7, [pltpu.VMEM((256, 128), F32)]
    )(oq, oq_other, dkv, lax.all_gather(theirs, "xl"), gate, go, w_proj)
    (pair_gradient,) = call(final_kernel, [((4, 128, 128), BF16)], 0, 3)(
        pair, gain, lax.all_gather(part, "c")
    )
    return jnp.swapaxes(out, 1, 2), pair_gradient


def solution(mesh):
    fine = Mesh(np.asarray(mesh.devices).reshape(2, 4, 2, 16, 2), ("xh", "y", "xl", "z", "c"))
    row, col = ("xh", "y"), ("xl", "z")
    return jax.shard_map(
        per_device,
        mesh=fine,
        in_specs=(
            P(row, col, None),
            P(),
            P(None, "c"),
            P("c", None),
            P("c", col, row),
            P(),
            P(row, col, None),
        ),
        out_specs=(P(row, col, "c"), P(row, col, None)),
        check_vma=False,
    )
```

```python
import functools

import jax
import jax.numpy as jnp
import numpy as np
from jax import lax
from jax.experimental import pallas as pl
from jax.experimental.pallas import tpu as pltpu
from jax.sharding import Mesh
from jax.sharding import PartitionSpec as P

DH = 32
SCALE = DH ** (-0.5)
EPS = 1e-05
NEG = -1e30
F32 = jnp.float32
BF16 = jnp.bfloat16
SWAP = [(0, 1), (1, 0)]
OWN, UP, DOWN, UP2, DOWN2 = range(5)
ARRAYS = ((0, 0, 4), (1, 0, 4), (-1, 0, 4), (2, 0, 2), (-2, 2, 2))


def place():
    return [lax.axis_index(name) for name in ("z", "xl", "c")]


def vmem():
    return pl.BlockSpec(memory_space=pltpu.VMEM)


def smem():
    return pl.BlockSpec(memory_space=pltpu.SMEM)


def shapes(*items):
    return [jax.ShapeDtypeStruct(s, d) for s, d in items]


def call(kernel, outs, n_smem, n_vmem, scratch=(), flops=0, nbytes=0):
    return pl.pallas_call(
        kernel,
        out_shape=shapes(*outs),
        in_specs=[smem()] * n_smem + [vmem()] * n_vmem,
        out_specs=[vmem()] * len(outs),
        scratch_shapes=list(scratch),
        compiler_params=pltpu.CompilerParams(vmem_limit_bytes=24 * 1024 * 1024),
        cost_estimate=pl.CostEstimate(flops=flops, bytes_accessed=nbytes, transcendentals=0),
    )


def nt(a, b):
    return lax.dot_general(a, b, (((1,), (1,)), ((), ())), preferred_element_type=F32)


def nn(a, b):
    return jnp.dot(a, b, preferred_element_type=F32)


def norm(x):
    mean = jnp.mean(x, axis=-1, keepdims=True)
    centred = x - mean
    inv = lax.rsqrt(jnp.mean(centred * centred, axis=-1, keepdims=True) + EPS)
    return centred * inv, inv


def make_lists(ids, act, lists):
    for k, (step, low, count) in enumerate(ARRAYS):
        for half in range(2):
            a = tile_of(ids[0], ids[1] if half == 0 else 1 - ids[1])
            base = 9 * (2 * k + half)
            n = 0
            for u in range(2 * count):
                zk = (ids[0] + step + 16) % 4 + 4 * (u // 2 + low)
                xk = ids[1] if u % 2 == 0 else 1 - ids[1]
                lists[base + n] = u
                n = n + act[a, tile_of(zk, xk)]
            lists[base + 8] = n


def bias_kernel(here, out, bias, sem):
    copy = pltpu.make_async_copy(here, bias, sem)
    copy.start()
    copy.wait()
    for j in range(4):
        for h in range(2):
            block = bias[h, :, 128 * j : 128 * j + 128].T
            out[h, j] = block
            out[2 + h, j] = block


def prep_kernel(*refs):
    ids = place()
    here, (keep, send, gate_out, go_out, lists) = refs[:6], refs[7:12]
    pair, gain, w_proj, w_out, d_out, act = local = refs[12:18]
    proj_s, sems = refs[18:]
    copies = [pltpu.make_async_copy(s, d, sems.at[k]) for k, (s, d) in enumerate(zip(here, local))]
    for copy in reversed(copies):
        copy.start()
    copies[5].wait()
    make_lists(ids, act, lists)
    for copy in copies[:5]:
        copy.wait()
    xl = ids[1]
    w_t = w_proj[...].T
    for p in range(2):
        for i in range(2):
            r = 2 * p + i
            xhat, _ = norm(pair[r].astype(F32))
            normed = (xhat * gain[...]).astype(BF16)
            proj = nt(w_t, normed)
            go = nt(w_out[...], d_out[r])
            go_out[r] = go
            for h in range(2):
                gate = jax.nn.sigmoid(proj[h * 128 + 96 : h * 128 + 128])
                gate_out[r, h * DH : (h + 1) * DH] = gate
                proj_s[h, i * 64 : (i + 1) * 64] = proj[h * 128 + 32 : h * 128 + 96]
                proj_s[h, 128 + i * 64 : 160 + i * 64] = proj[h * 128 : h * 128 + 32] * SCALE
                proj_s[h, 160 + i * 64 : 192 + i * 64] = go[h * DH : (h + 1) * DH] * gate
        for ref, h in ((keep, xl), (send, 1 - xl)):
            ref[p * 128 : (p + 1) * 128] = proj_s[h, 0:128].T.astype(BF16)
            ref[256 + p * 128 : 384 + p * 128] = proj_s[h, 128:256].astype(BF16)


def fill_queries(qd, packs):
    qd[...] = jnp.zeros_like(qd)
    for half, pack in enumerate(packs):
        for r in range(4):
            low = 64 * (r % 2)
            qd[half, r, low : low + 32, 0:128] = pack[256 + 64 * r : 288 + 64 * r]
            qd[half, r, low + 32 : low + 64, 128:256] = pack[288 + 64 * r : 320 + 64 * r]


def tile_of(zk, xk):
    return zk // 2 + 8 * xk


def setup_kernel(pack0, pack1, qd, kv):
    for p in range(2):
        kv[0, p] = pack0[128 * p : 128 * p + 128]
        kv[1, p] = pack1[128 * p : 128 * p + 128]
    fill_queries(qd, (pack0, pack1))


def load_units(ids, kv, bias, which, half, units):
    step, low, _ = ARRAYS[which]
    keys = [[kv[u // 2, u % 2, p] for u in units] for p in range(2)]
    b = []
    for u in units:
        xk = jnp.where(u % 2 == 0, ids[1], 1 - ids[1])
        xq = jnp.where(half == 0, ids[1], 1 - ids[1])
        b.append(bias[u // 2 + low, xk, xq, (ids[0] + step + 16) % 4].astype(F32))
    keys = [k[0] if len(k) == 1 else jnp.concatenate(k, axis=0) for k in keys]
    return keys, b[0] if len(b) == 1 else jnp.concatenate(b, axis=0)


def over_units(lists, which, half, body):
    base = 9 * (2 * which + half)
    n = lists[base + 8]

    @pl.loop(0, n // 4)
    def _(k):
        body([lists[base + 4 * k + j] for j in range(4)])

    @pl.when(n % 4 >= 2)
    def _():
        body([lists[base + n // 4 * 4], lists[base + n // 4 * 4 + 1]])

    @pl.when(n % 2 == 1)
    def _():
        body([lists[base + n - 1]])


def stats_kernel(names, begin, end, lists, *refs):
    n, ids = len(names), place()
    kvs, (bias, qd), refs = refs[:n], refs[n : n + 2], refs[n + 2 :]
    before, refs = (None, refs) if begin else (refs[0], refs[1:])
    out, st = refs
    if begin:
        st[0] = jnp.full(st.shape[1:], NEG, F32)
        st[1:3] = jnp.zeros((2,) + st.shape[1:], F32)
    else:
        st[...] = before[...]

    @pl.loop(0, 2)
    def _(half):
        for kv, which in zip(kvs, names):

            def body(units, kv=kv, which=which):
                keys, b = load_units(ids, kv, bias, which, half, units)
                for r in range(4):
                    sd = nn(keys[r // 2], qd[half, r])
                    m, l, d = (st[k, half, r] for k in range(3))
                    for low in range(0, b.shape[0], 64):
                        rows = slice(low, low + 64)
                        s = (sd[rows, :128] + b[rows]).reshape(-1, 8, 128)
                        dp = sd[rows, 128:].reshape(-1, 8, 128)
                        m_new = jnp.maximum(m, jnp.max(s, axis=0))
                        e = jnp.exp(s - m_new[None])
                        c = jnp.exp(m - m_new)
                        m, l, d = m_new, l * c + jnp.sum(e, axis=0), d * c + jnp.sum(e * dp, axis=0)
                    st[0, half, r], st[1, half, r], st[2, half, r] = m, l, d

            over_units(lists, which, half, body)

    if not end:
        out[...] = st[...]
        return
    for half in range(2):
        for r in range(4):
            m = st[0, half, r]
            top = jnp.max(m, axis=0, keepdims=True)
            f = jnp.exp(m - top)
            total = jnp.sum(st[1, half, r] * f, axis=0, keepdims=True)
            out[half, r, 0:1] = top + jnp.log(total)
            out[half, r, 1:2] = jnp.sum(st[2, half, r] * f, axis=0, keepdims=True) / total


def back_kernel(names, lists, *refs):
    n, ids = len(names), place()
    kvs, (bias, qd, stats) = refs[:n], refs[n : n + 3]
    dkvs, (oq, acc) = refs[n + 3 : 2 * n + 3], refs[2 * n + 3 :]
    oq[...] = jnp.zeros_like(oq)
    for kv, dkv, which in zip(kvs, dkvs, names):
        count = kv.shape[0]
        acc[0:count] = jnp.zeros((count,) + acc.shape[1:], F32)

        @pl.loop(0, 2)
        def _(half):
            def body(units):
                keys, b = load_units(ids, kv, bias, which, half, units)
                for p in range(2):
                    keys_t = keys[p].T
                    qs = [qd[half, 2 * p + i] for i in range(2)]
                    sd = [nn(keys[p], q) for q in qs]
                    pds = []
                    for i in range(2):
                        r = 2 * p + i
                        prob = jnp.exp(sd[i][:, :128] + (b - stats[half, r, 0:1]))
                        dsc = prob * (sd[i][:, 128:] - stats[half, r, 1:2])
                        pds.append(jnp.concatenate([dsc.astype(BF16), prob.astype(BF16)], axis=1))
                    both = nt(jnp.concatenate(pds, axis=1), jnp.concatenate(qs, axis=1))
                    for k, u in enumerate(units):
                        acc[u // 2, u % 2, p] += both[128 * k : 128 * k + 128]
                    for i in range(2):
                        r = 2 * p + i
                        t = nn(keys_t[64 * i : 64 * i + 64], pds[i])
                        oq[half, r, 0:32] += t[0:32, 0:128]
                        oq[half, r, 32:64] += t[32:64, 128:256]

            over_units(lists, which, half, body)

        dkv[...] = acc[0:count].astype(BF16)


def mid_kernel(lists, up2, down2, up, down, bias, qd, before, stats, d_up, d_down, oq, st, acc):
    stats_kernel((UP2, DOWN2), False, True, lists, up2, down2, bias, qd, before, stats, st)
    back_kernel((UP, DOWN), lists, up, down, bias, qd, stats, d_up, d_down, oq, acc)


def out_kernel(oq_own, oq_other, gate, w_out, keep, send):
    _, xl, c = place()
    w_t = w_out[...].T
    for r in range(4):
        mine, theirs = oq_own[0, r, 32:64], oq_other[r, 32:64].astype(F32)
        att = jnp.concatenate(
            [jnp.where(xl == 0, mine, theirs), jnp.where(xl == 0, theirs, mine)], axis=0
        )
        part = nn(w_t, (gate[r] * att).astype(BF16))
        low, high = part[0:64], part[64:128]
        keep[r] = jnp.where(c == 0, low, high)
        send[r] = jnp.where(c == 0, high, low).astype(BF16)


def sum_kernel(d_own, r_up, r_down, r_up2, r_down2, out):
    for m in range(4):
        total = d_own[m].astype(F32) + r_up[m].astype(F32) + r_down[m].astype(F32)
        total += (r_up2[m] if m < 2 else r_down2[m - 2]).astype(F32)
        out[m] = total.astype(BF16)


def proj_kernel(oq_own, oq_other, dkv_own, dkv_other, gate, go, w_proj, send, dp):
    _, xl, _ = place()
    for p in range(2):
        mine_kv = sum(dkv_own[m, 0, p].astype(F32) for m in range(4)).T
        theirs_kv = dkv_other[1 - xl, p].astype(F32).T
        for i in range(2):
            r = 2 * p + i
            for oq, kvt, h in (
                (oq_own[0, r], mine_kv, xl),
                (oq_other[r].astype(F32), theirs_kv, 1 - xl),
            ):
                low = pl.multiple_of(h * DH, DH)
                g = gate[r, pl.ds(low, DH)]
                base = pl.multiple_of(h * 128, 128)
                dp[pl.ds(base, 32)] = oq[0:32]
                dp[pl.ds(base + 32, 64)] = kvt[64 * i : 64 * i + 64]
                dp[pl.ds(base + 96, 32)] = go[r, pl.ds(low, DH)] * oq[32:64] * g * (1.0 - g)
            send[r] = nn(w_proj[...], dp[...].astype(BF16)).T.astype(BF16)


def final_kernel(pair, gain, parts, out):
    for r in range(4):
        xhat, inv = norm(pair[r].astype(F32))
        g = (parts[0, r].astype(F32) + parts[1, r].astype(F32)) * gain[...]
        mean = jnp.mean(g, axis=-1, keepdims=True)
        along = jnp.mean(g * xhat, axis=-1, keepdims=True)
        out[r] = (inv * (g - mean - xhat * along)).astype(BF16)


def stats_call(names, begin, end, lists, kvs, rest):
    out = ((2, 4, 2, 128), F32) if end else ((3, 2, 4, 8, 128), F32)
    return call(
        functools.partial(stats_kernel, names, begin, end),
        [out],
        1,
        len(kvs) + len(rest),
        [pltpu.VMEM((3, 2, 4, 8, 128), F32)],
        flops=10 ** 9,
        nbytes=10 ** 7,
    )(lists, *kvs, *rest)[0]


def back_call(names, lists, kvs, rest):
    res = call(
        functools.partial(back_kernel, names),
        [(kv.shape, BF16) for kv in kvs] + [((2, 4, 64, 128), F32)],
        1,
        len(kvs) + len(rest),
        [pltpu.VMEM((4, 2, 2, 128, 128), F32)],
        flops=2 * 10 ** 9,
        nbytes=2 * 10 ** 7,
    )(lists, *kvs, *rest)
    return res[:-1], res[-1]


def to_z(x, step):
    return lax.ppermute(x, "z", [(j, (j + step) % 16) for j in range(16)])


def per_device(pair, gain, w_proj, w_out, tri_bias, active, d_out):
    gain = gain.reshape(1, 128)
    whole = pl.BlockSpec(memory_space=pl.ANY)
    big = pltpu.CompilerParams(vmem_limit_bytes=56 * 1024 * 1024)
    bias = pl.pallas_call(
        bias_kernel,
        out_shape=jax.ShapeDtypeStruct((4, 4, 128, 128), BF16),
        in_specs=[whole],
        out_specs=vmem(),
        scratch_shapes=[pltpu.VMEM(tri_bias.shape, BF16), pltpu.SemaphoreType.DMA(())],
        compiler_params=big,
    )(tri_bias)
    args = (pair, gain, w_proj, w_out, d_out, active)
    pack, pack_send, gate, go, lists = pl.pallas_call(
        prep_kernel,
        out_shape=shapes(
            *[((512, 128), BF16)] * 2, *[((4, 64, 128), F32)] * 2, ((90,), jnp.int32)
        ),
        in_specs=[whole] * 7,
        out_specs=[vmem()] * 4 + [smem()],
        scratch_shapes=[pltpu.VMEM(a.shape, a.dtype) for a in args[:5]]
        + [pltpu.SMEM(active.shape, active.dtype)]
        + [pltpu.VMEM((2, 256, 128), F32), pltpu.SemaphoreType.DMA((6,))],
        compiler_params=big,
    )(*args, bias)
    pack_other = lax.ppermute(pack_send, "xl", SWAP)
    bias = lax.all_to_all(bias, ("xh", "xl"), 0, 0, tiled=True).reshape(2, 2, 4, 128, 128)
    bias, pack_other = lax.optimization_barrier((bias, pack_other))
    bias = lax.all_gather(bias, "y")
    qd, kv = call(
        setup_kernel, [((2, 4, 128, 256), BF16), ((2, 2, 128, 128), BF16)], 0, 2
    )(pack, pack_other)
    groups = [[k + 4 * m for m in range(4)] for k in range(4)]
    own = lax.all_gather(kv, "z", axis_index_groups=groups)
    up, down = to_z(own, -1), to_z(own, 1)
    up2, down2 = to_z(own[0:2], -2), to_z(own[2:4], 2)
    rest = (bias, qd)
    state = stats_call((OWN,), True, False, lists, (own,), rest)
    state = stats_call((UP, DOWN), False, False, lists, (up, down), rest + (state,))
    stats, d_up, d_down, oq1 = call(
        mid_kernel,
        [((2, 4, 2, 128), F32), (up.shape, BF16), (down.shape, BF16), ((2, 4, 64, 128), F32)],
        1,
        7,
        [pltpu.VMEM((3, 2, 4, 8, 128), F32), pltpu.VMEM((4, 2, 2, 128, 128), F32)],
        flops=3 * 10 ** 9,
        nbytes=3 * 10 ** 7,
    )(lists, up2, down2, up, down, bias, qd, state)
    r_up, r_down = to_z(d_up, 1), to_z(d_down, -1)
    rest = rest + (stats,)
    (d_up2, d_down2), oq2 = back_call((UP2, DOWN2), lists, (up2, down2), rest)
    r_up2, r_down2 = to_z(d_up2, 2), to_z(d_down2, -2)
    (d_own,), oq0 = back_call((OWN,), lists, (own,), rest)
    oq = oq0 + oq1 + oq2
    oq = jnp.concatenate([oq[:, :, :32] * SCALE, oq[:, :, 32:]], axis=2)
    oq_other = lax.ppermute(oq[1].astype(BF16), "xl", SWAP)
    out_keep, out_send = call(
        out_kernel, [((4, 64, 128), F32), ((4, 64, 128), BF16)], 0, 4
    )(oq, oq_other, gate, w_out)
    out_other = lax.ppermute(out_send, "c", SWAP)
    out = (out_keep + out_other.astype(F32)).astype(BF16)
    (sums,) = call(sum_kernel, [((4, 2, 2, 128, 128), BF16)], 0, 5)(
        d_own, r_up, r_down, r_up2, r_down2
    )
    dkv = lax.all_to_all(sums, "z", 0, 0, axis_index_groups=groups, tiled=True)
    dkv, out = lax.optimization_barrier((dkv, out))
    theirs = jnp.sum(dkv[:, 1].astype(F32), axis=0).astype(BF16)
    (part,) = call(
        proj_kernel, [((4, 128, 128), BF16)], 0, 7, [pltpu.VMEM((256, 128), F32)]
    )(oq, oq_other, dkv, lax.all_gather(theirs, "xl"), gate, go, w_proj)
    (pair_gradient,) = call(final_kernel, [((4, 128, 128), BF16)], 0, 3)(
        pair, gain, lax.all_gather(part, "c")
    )
    return jnp.swapaxes(out, 1, 2), pair_gradient


def solution(mesh):
    fine = Mesh(np.asarray(mesh.devices).reshape(2, 4, 2, 16, 2), ("xh", "y", "xl", "z", "c"))
    row, col = ("xh", "y"), ("xl", "z")
    return jax.shard_map(
        per_device,
        mesh=fine,
        in_specs=(
            P(row, col, None),
            P(),
            P(None, "c"),
            P("c", None),
            P("c", col, row),
            P(),
            P(row, col, None),
        ),
        out_specs=(P(row, col, "c"), P(row, col, None)),
        check_vma=False,
    )
```
